32 devices in a mesh: clus: 8 (over y, x, core), sub: 4 (over z).
Axes of the slice: x: 2, y: 2, z: 4, core: 2. Of those that a mesh axis runs over, the one named last changes fastest.
Arguments:
- schur: bfloat16 [8, 4, 512, 512], P('clus', 'sub'), as said below
- load: float32 [8, 4, 4, 16, 128], P('clus', 'sub')
- rigid: float32 [8, 4, 4, 6, 128], P('clus', 'sub')
- lengths: int32 [8, 4, 4], P('clus', 'sub'), may hold values from 0 to 128, as said below
- partner: int32 [8, 4, 4, 128], P('clus', 'sub'), may hold values from 0 to 127, as said below
- coarse_inverse: float32 [48, 48], replicated, as said below
Outputs:
- multipliers: float32 [8, 4, 4, 16, 128], P('clus', 'sub')
- residual: float32 [8, 4, 4, 16, 128], P('clus', 'sub')
The draws below stay inside these ranges and needn't reach their ends.
Inputs may be any that keep to these rules, and one draw needn't show every extreme that they name: `schur`: each subdomain's matrix is symmetric. `coarse_inverse`: symmetric. `lengths`: both sides of a neighbour pair hold the same length; 0 exactly where no neighbour exists; some pair has 128. On used rows, partner maps the used rows of a pair one to one onto the neighbour's used rows of the opposite direction, and the neighbour's partner maps them back; unused rows hold their own index.
All inputs are finite; a program needn't handle non-finite values.
Results may differ from the reference program's by a relative error of at most 0.0039.
Values sent between devices are 32-bit elements; how exact they have to be, the bound alone decides.
No kernel may reach another device: no remote copies, remote signals or barrier semaphores. Data moves between devices by JAX's collectives and lax.ppermute only.
A program may use at most 64 MiB of HBM per device.

```python
import math
import jax
import jax.numpy as jnp
from jax import lax

PAIR = 128
CASES = 16
MODES = 6
ITERS = 2
NCL = 8
NSUB = 4
COARSE = 48
N_CLUS = 8
N_SUB = 4


def symmetric_block(key, count, order, low, high):
    key_off, key_diag = jax.random.split(key, 2)
    bound = 0.52 / math.sqrt(order)
    raw_part = jax.random.uniform(key_off, (count, order, order), jnp.float32, -bound, bound)
    off_part = (raw_part + jnp.swapaxes(raw_part, 1, 2)) * (1.0 / math.sqrt(2.0))
    eye_mat = jnp.eye(order, dtype=jnp.float32)
    diag_part = jax.random.uniform(key_diag, (count, order), jnp.float32, low, high)
    matrix = off_part * (1.0 - eye_mat) + eye_mat * diag_part[:, :, None]
    return matrix


def draw_schur(key, part):
    cluster_keys = jax.random.split(jax.random.fold_in(key, 101), NCL)

    def one_cluster(cluster_key):
        return symmetric_block(cluster_key, NSUB, 4 * PAIR, 1.0, 2.0).astype(jnp.bfloat16)
    return lax.map(one_cluster, cluster_keys)


def draw_coarse_inverse(key, part):
    return symmetric_block(jax.random.fold_in(key, 202), 1, COARSE, 0.8, 1.6)[0]


def rigid_modes(key):
    base_key = jax.random.fold_in(key, 303)
    shape = (NCL, NSUB, 4, MODES, PAIR)
    scale = 1.0 / math.sqrt(NSUB * 4 * PAIR)
    return jax.random.normal(base_key, shape, jnp.float32) * scale


def draw_rigid(key, part):
    return rigid_modes(key)


def draw_load(key, part):
    modes_part = rigid_modes(key)
    key_noise, key_mix = jax.random.split(jax.random.fold_in(key, 404))
    shape = (NCL, NSUB, 4, CASES, PAIR)
    cluster_rise = 0.5 + jnp.arange(NCL, dtype=jnp.float32) / max(NCL - 1, 1)
    noise = jax.random.normal(key_noise, shape, jnp.float32)
    mixing = jax.random.normal(key_mix, (NCL, MODES, CASES), jnp.float32) * (1.0 / math.sqrt(MODES))
    aligned = jnp.einsum('csdmp,cmj->csdjp', modes_part, mixing) * math.sqrt(NSUB * 4 * PAIR)
    return noise * cluster_rise[:, None, None, None, None] + aligned


def edge_tables(key):
    base_key = jax.random.fold_in(key, 55)
    key_len_sub, key_len_clus, key_score_sub, key_score_clus = jax.random.split(base_key, 4)
    len_sub = jax.random.randint(key_len_sub, (NCL, NSUB), PAIR // 4, PAIR + 1).astype(jnp.int32)
    len_sub = len_sub.at[0, 0].set(PAIR)
    len_clus = jax.random.randint(key_len_clus, (NCL, NSUB), PAIR // 4, PAIR + 1).astype(jnp.int32)
    row_ids = jnp.arange(PAIR, dtype=jnp.int32)

    def matchings(score_key, edge_len):
        score = jax.random.randint(score_key, edge_len.shape + (PAIR,), 0, 65536).astype(jnp.int32) * PAIR + row_ids
        score = jnp.where(row_ids < edge_len[..., None], score, 1073741824 + row_ids)
        forward = jnp.argsort(score, axis=-1).astype(jnp.int32)
        backward = jnp.argsort(forward, axis=-1).astype(jnp.int32)
        return (forward, backward)
    fwd_sub, back_sub = matchings(key_score_sub, len_sub)
    fwd_clus, back_clus = matchings(key_score_clus, len_clus)
    zero_sub = jnp.zeros((NCL, 1), jnp.int32)
    zero_clus = jnp.zeros((1, NSUB), jnp.int32)
    len_lo_sub = jnp.concatenate([zero_sub, len_sub[:, :-1]], axis=1)
    len_hi_sub = jnp.concatenate([len_sub[:, :-1], zero_sub], axis=1)
    len_lo_clus = jnp.concatenate([zero_clus, len_clus[:-1]], axis=0)
    len_hi_clus = jnp.concatenate([len_clus[:-1], zero_clus], axis=0)
    all_lengths = jnp.stack([len_lo_sub, len_hi_sub, len_lo_clus, len_hi_clus], axis=2)
    ident_sub = jnp.broadcast_to(row_ids, (NCL, 1, PAIR))
    ident_clus = jnp.broadcast_to(row_ids, (1, NSUB, PAIR))
    part_lo_sub = jnp.concatenate([ident_sub, back_sub[:, :-1]], axis=1)
    part_hi_sub = jnp.concatenate([fwd_sub[:, :-1], ident_sub], axis=1)
    part_lo_clus = jnp.concatenate([ident_clus, back_clus[:-1]], axis=0)
    part_hi_clus = jnp.concatenate([fwd_clus[:-1], ident_clus], axis=0)
    all_partners = jnp.stack([part_lo_sub, part_hi_sub, part_lo_clus, part_hi_clus], axis=2)
    return (all_lengths, all_partners)


def draw_lengths(key, part):
    return edge_tables(key)[0]


def draw_partner(key, part):
    return edge_tables(key)[1]


def setup_inputs(seed: int = 0) -> dict:
    streams_of = jax.random.split(jax.random.key(seed), 7)
    schur = draw_schur(jax.random.fold_in(streams_of[6], 71), 0)
    load = draw_load(jax.random.fold_in(streams_of[6], 71), 0)
    rigid = draw_rigid(jax.random.fold_in(streams_of[6], 71), 0)
    lengths = draw_lengths(jax.random.fold_in(streams_of[6], 71), 0)
    partner = draw_partner(jax.random.fold_in(streams_of[6], 71), 0)
    coarse_inverse = draw_coarse_inverse(jax.random.fold_in(streams_of[6], 71), 0)
    return dict(schur=schur, load=load, rigid=rigid, lengths=lengths, partner=partner, coarse_inverse=coarse_inverse)


FULL_PRECISION = lax.Precision.HIGHEST


def sign_table():
    return jnp.array([-1.0, 1.0, -1.0, 1.0], jnp.float32)


def far_side(values, partner):
    zero_sub = jnp.zeros_like(values[:, :1, 0])
    zero_clus = jnp.zeros_like(values[:1, :, 0])
    lower_sub = jnp.concatenate([zero_sub, values[:, :-1, 1]], axis=1)
    upper_sub = jnp.concatenate([values[:, 1:, 0], zero_sub], axis=1)
    lower_clus = jnp.concatenate([zero_clus, values[:-1, :, 3]], axis=0)
    upper_clus = jnp.concatenate([values[1:, :, 2], zero_clus], axis=0)
    arrived = jnp.stack([lower_sub, upper_sub, lower_clus, upper_clus], axis=2)
    gather_index = jnp.broadcast_to(partner[:, :, :, None, :], arrived.shape)
    return jnp.take_along_axis(arrived, gather_index, axis=4)


def reference(schur, load, rigid, lengths, partner, coarse_inverse):
    slot_index = lax.broadcasted_iota(jnp.int32, (N_CLUS, N_SUB, 4, PAIR), 3)
    live_rows = (slot_index < lengths[:, :, :, None]).astype(jnp.float32)
    sign_live = (sign_table()[None, None, :, None] * live_rows)[:, :, :, None, :]

    def jump_rows(values):
        return sign_live * (values - far_side(values, partner))

    diag_own = jnp.diagonal(schur, axis1=2, axis2=3).astype(jnp.float32).reshape(N_CLUS, N_SUB, 4, 1, PAIR)
    weight = live_rows[:, :, :, None, :] / (diag_own + far_side(diag_own, partner))
    dual_rhs = jump_rows(load)
    signed_rigid = rigid * sign_live

    def project(vector):
        coarse_sums = jnp.einsum("csdmp,csdjp->cmj", signed_rigid, vector, precision=FULL_PRECISION)
        coeffs = jnp.dot(coarse_inverse, coarse_sums.reshape(N_CLUS * MODES, CASES), precision=FULL_PRECISION)
        coeffs = coeffs.reshape(N_CLUS, MODES, CASES)
        expanded = jnp.einsum("csdmp,cmj->csdjp", rigid, coeffs, precision=FULL_PRECISION)
        return vector - jump_rows(expanded)

    def inner_dot(left_vec, right_vec):
        return 0.5 * jnp.sum(left_vec * right_vec, axis=(0, 1, 2, 4))

    def cluster_apply(pair_args):
        matrices, vectors = pair_args
        flattened = vectors.astype(jnp.float32).transpose(0, 2, 1, 3).reshape(N_SUB, CASES, 4 * PAIR)
        image_rows = jnp.einsum("sji,siq->sjq", flattened, matrices.astype(jnp.float32), precision=FULL_PRECISION)
        return image_rows.reshape(N_SUB, CASES, 4, PAIR).transpose(0, 2, 1, 3)

    def apply_schur(direction):
        operand = (sign_live * direction).astype(jnp.bfloat16)
        image_rows = lax.map(cluster_apply, (schur, operand))
        return jump_rows(image_rows)

    multipliers = jnp.zeros_like(load)
    residual = dual_rhs
    direction = jnp.zeros_like(load)
    rho_old = jnp.ones((CASES,), jnp.float32)
    for iteration in range(ITERS):
        projected = project(residual)
        precond = project(weight * projected)
        rho_now = inner_dot(projected, precond)
        if iteration == 0:
            direction = precond
        else:
            direction = precond + (rho_now / rho_old)[:, None] * direction
        image_rows = apply_schur(direction)
        step_size = rho_now / inner_dot(direction, image_rows)
        multipliers = multipliers + step_size[:, None] * direction
        residual = residual - step_size[:, None] * image_rows
        rho_old = rho_now
    return multipliers, residual
```

```python
import jax
import jax.numpy as jnp
from jax import lax
from jax.sharding import PartitionSpec as P

AXES = ("clus", "sub")
PRECISION = lax.Precision.HIGHEST


def pair_even(index, count):
    other = index ^ 1
    return other if other < count else index


def pair_odd(index, count):
    other = ((index - 1) ^ 1) + 1
    return other if index > 0 and other < count else index


def swap_tables(clusters, subs):
    clus_even, clus_odd, sub_even, sub_odd = [], [], [], []
    for c in range(clusters):
        for s in range(subs):
            here = c * subs + s
            clus_even.append((here, pair_even(c, clusters) * subs + s))
            odd = pair_odd(c, clusters)
            target = odd * subs + s if odd != c else c * subs + pair_even(s, subs)
            clus_odd.append((here, target))
            sub_even.append((here, c * subs + pair_even(s, subs)))
            odd = pair_odd(s, subs)
            target = c * subs + odd if odd != s else pair_even(c, clusters) * subs + s
            sub_odd.append((here, target))
    return clus_even, clus_odd, sub_even, sub_odd


def exchange(values):
    clusters, subs = lax.axis_size("clus"), lax.axis_size("sub")
    clus_even, clus_odd, sub_even, sub_odd = swap_tables(clusters, subs)
    even_c = lax.axis_index("clus") % 2 == 0
    even_s = lax.axis_index("sub") % 2 == 0
    by_sub_even = lax.ppermute(jnp.where(even_s, values[1], values[0]), AXES, sub_even)
    by_sub_odd = lax.ppermute(jnp.where(even_s, values[0], values[1]), AXES, sub_odd)
    by_clus_odd = lax.ppermute(jnp.where(even_c, values[2], values[3]), AXES, clus_odd)
    by_clus_even = lax.ppermute(jnp.where(even_c, values[3], values[2]), AXES, clus_even)
    return jnp.stack([
        jnp.where(even_s, by_sub_odd, by_sub_even),
        jnp.where(even_s, by_sub_even, by_sub_odd),
        jnp.where(even_c, by_clus_odd, by_clus_even),
        jnp.where(even_c, by_clus_even, by_clus_odd),
    ])


def dot(left, right):
    return jnp.dot(left, right, precision=PRECISION)


def to_all(packed):
    count = lax.axis_size("clus") * lax.axis_size("sub")
    copies = jnp.broadcast_to(packed[None], (count, packed.shape[0]))
    return lax.all_to_all(copies, AXES, 0, 0, tiled=True)


def shards(schur, load, rigid, lengths, partner, coarse_inverse):
    own_load = load[0, 0]
    cases, pair_rows = own_load.shape[1], own_load.shape[2]
    rig_own = rigid[0, 0]
    modes = rig_own.shape[1]
    matrix = schur[0, 0]
    clusters, subs = lax.axis_size("clus"), lax.axis_size("sub")
    cluster_at = lax.axis_index("clus")
    rows = 4 * pair_rows

    table = (partner[0, 0][:, :, None] == lax.broadcasted_iota(jnp.int32, (4, pair_rows, pair_rows), 2))
    table = table.astype(jnp.float32)
    live = (lax.broadcasted_iota(jnp.int32, (4, pair_rows), 1) < lengths[0, 0][:, None])[:, None, :]
    sign = jnp.array([-1.0, 1.0, -1.0, 1.0], jnp.float32)[:, None, None]
    sign_live = sign * live.astype(jnp.float32)
    diag_mask = lax.broadcasted_iota(jnp.int32, (rows, rows), 0) == lax.broadcasted_iota(jnp.int32, (rows, rows), 1)
    diag_own = jnp.sum(jnp.where(diag_mask, matrix, 0).astype(jnp.float32), axis=0).reshape(4, 1, pair_rows)

    def far(values):
        return jnp.einsum("djq,dkq->djk", exchange(values), table, precision=PRECISION)

    def flat(values):
        return jnp.swapaxes(values, 0, 1).reshape(values.shape[1], rows)

    def unflat(values):
        return jnp.swapaxes(values.reshape(values.shape[0], 4, pair_rows), 0, 1)

    matrix32 = matrix.astype(jnp.float32)

    far_first = far(jnp.concatenate([own_load, rig_own, diag_own], axis=1))
    far_load = far_first[:, :cases]
    far_rigid = far_first[:, cases:cases + modes]
    far_diag = far_first[:, cases + modes:]
    weight = jnp.where(live, 1.0 / jnp.where(live, diag_own + far_diag, 1.0), 0.0)
    rhs = sign_live * (own_load - far_load)
    zero = jnp.zeros_like(rig_own[0])
    near = jnp.concatenate([rig_own[:2] - far_rigid[:2], rig_own[2:]])
    low = jnp.stack([zero, zero, -far_rigid[2], zero])
    high = jnp.stack([zero, zero, zero, -far_rigid[3]])
    basis = sign_live * jnp.concatenate([low, near, high], axis=1)
    weighted_basis = weight * basis
    weighted_rhs = weight * rhs

    operand = flat(sign_live * jnp.concatenate([weighted_basis, basis, weighted_rhs], axis=1))
    image = dot(operand, matrix32)
    span = 3 * modes
    gram = dot(operand[:2 * span], image.T)
    signed_rigid = flat(sign_live * rig_own)
    coarse_parts = dot(signed_rigid, flat(jnp.concatenate([rhs, weighted_rhs, weighted_basis], axis=1)).T)

    packed = jnp.concatenate([gram.reshape(-1), coarse_parts.reshape(-1)])
    gathered = to_all(packed).reshape(clusters, subs, -1)
    image_far = far(unflat(image))

    sums = jnp.sum(gathered, axis=1)
    gram_all = sums[:, :gram.size].reshape(clusters, 2 * span, 2 * span + cases)
    coarse_all = sums[:, gram.size:].reshape(clusters, modes, 2 * cases + span)

    order = clusters * modes
    tall = (clusters + 2) * modes

    def solve(values):
        return dot(coarse_inverse, values)

    def padded(values):
        return jnp.pad(values, ((modes, modes), (0, 0)))

    def near_coeffs(values):
        return jnp.stack([values[c * modes:c * modes + span] for c in range(clusters)])

    coupling = coarse_all[:, :, 2 * cases:]

    def couple(values):
        product = jnp.einsum("cmk,ckj->cmj", coupling, near_coeffs(padded(values)), precision=PRECISION)
        return product.reshape(order, cases)

    first_a = solve(coarse_all[:, :, :cases].reshape(order, cases))
    first_b = solve(coarse_all[:, :, cases:2 * cases].reshape(order, cases) - couple(first_a))
    near_first = jnp.concatenate([near_coeffs(padded(first_a)), near_coeffs(padded(first_b))], axis=1)
    parts = gram_all[:, :, 2 * span:] - jnp.einsum(
        "cik,ckj->cij", gram_all[:, :, :2 * span], near_first, precision=PRECISION
    )

    def assemble(values):
        total = jnp.zeros((tall, cases), jnp.float32)
        for c in range(clusters):
            total = total.at[c * modes:c * modes + span].add(values[c])
        return total[modes:modes + order]

    second_a = solve(assemble(parts[:, span:]))
    second_b = solve(assemble(parts[:, :span]) - couple(second_a))

    def local(values, shift):
        wide = jnp.pad(values, ((2 * modes, 2 * modes), (0, 0)))
        return lax.dynamic_slice_in_dim(wide, (cluster_at + 1 + shift) * modes, span, 0)

    def combine(coeffs, block):
        return jnp.einsum("kj,dkp->djp", coeffs, block, precision=PRECISION)

    def combine_one(coeffs, block):
        return jnp.einsum("kj,kp->jp", coeffs, block, precision=PRECISION)

    a_zero, b_zero = local(first_a, 0), local(first_b, 0)
    c_zero = jnp.concatenate([a_zero, b_zero])
    c_low = jnp.concatenate([local(first_a, -1), local(first_b, -1)])
    c_high = jnp.concatenate([local(first_a, 1), local(first_b, 1)])
    a_one, b_one = local(second_a, 0), local(second_b, 0)

    projected = rhs - combine(a_zero, basis)
    first = weight * projected - combine(b_zero, basis)
    image_own = unflat(image)
    pair = 2 * span
    own_part = image_own[:, pair:] - combine(c_zero, image_own[:, :pair])
    far_sum = jnp.stack([
        combine_one(c_zero, image_far[0, :pair]),
        combine_one(c_zero, image_far[1, :pair]),
        combine_one(c_low, image_far[2, :pair]),
        combine_one(c_high, image_far[3, :pair]),
    ])
    far_part = image_far[:, pair:] - far_sum
    applied = sign_live * (own_part - far_part)
    applied_projected = applied - combine(a_one, basis)
    second = weight * applied_projected - combine(b_one, basis)

    second_operand = sign_live * second
    second_image = unflat(dot(flat(second_operand), matrix32))

    def half_dot(left, right):
        return 0.5 * jnp.sum(left * right, axis=(0, 2))

    scalars = jnp.concatenate([
        half_dot(projected, first),
        half_dot(first, applied),
        half_dot(projected, second) + half_dot(applied_projected, first),
        half_dot(applied_projected, second),
        half_dot(applied, second),
        jnp.sum(second_operand * second_image, axis=(0, 2)),
    ])
    totals = jnp.sum(to_all(scalars), axis=0).reshape(6, cases)
    second_far = far(second_image)
    rho_one, delta_one, cross, square, mixed, delta_second = [totals[i] for i in range(6)]
    second_applied = sign_live * (second_image - second_far)

    alpha_one = rho_one / delta_one
    rho_two = rho_one - alpha_one * cross + alpha_one * alpha_one * square
    beta = rho_two / rho_one
    grow = 1.0 + beta
    delta_two = grow * grow * delta_one - 2.0 * grow * alpha_one * mixed + alpha_one * alpha_one * delta_second
    alpha_two = rho_two / delta_two
    keep = (alpha_one + alpha_two * grow)[:, None]
    drop = (alpha_two * alpha_one)[:, None]
    multipliers = keep * first - drop * second
    residual = rhs - keep * applied + drop * second_applied
    return (multipliers[None, None], residual[None, None])


def solution(mesh):
    in_specs = (
        P("clus", "sub", None, None),
        P("clus", "sub", None, None, None),
        P("clus", "sub", None, None, None),
        P("clus", "sub", None),
        P("clus", "sub", None, None),
        P(),
    )
    out_specs = (P("clus", "sub", None, None, None), P("clus", "sub", None, None, None))
    return jax.shard_map(shards, mesh=mesh, in_specs=in_specs, out_specs=out_specs, check_vma=False)
```

```python
import functools

import jax
import jax.numpy as jnp
from jax import lax
from jax.experimental import pallas as pl
from jax.experimental.pallas import tpu as pltpu
from jax.sharding import PartitionSpec as P

AXES = ("clus", "sub")
F32 = jnp.float32
BF16 = jnp.bfloat16
FULL = lax.Precision.HIGHEST
STRIP = 8
PACK = 16
VMEM_LIMIT = 48 * 1024 * 1024


def pair_even(index, count):
    other = index ^ 1
    return other if other < count else index


def pair_odd(index, count):
    other = ((index - 1) ^ 1) + 1
    return other if index > 0 and other < count else index


def swap_tables(clusters, subs):
    sub_even, sub_odd, clus_odd, clus_even = [], [], [], []
    for c in range(clusters):
        for s in range(subs):
            here = c * subs + s
            sub_even.append((here, c * subs + pair_even(s, subs)))
            odd = pair_odd(s, subs)
            target = c * subs + odd if odd != s else pair_even(c, clusters) * subs + s
            sub_odd.append((here, target))
            odd = pair_odd(c, clusters)
            target = odd * subs + s if odd != c else c * subs + pair_even(s, subs)
            clus_odd.append((here, target))
            clus_even.append((here, pair_even(c, clusters) * subs + s))
    return sub_even, sub_odd, clus_odd, clus_even


def swap(buffers):
    tables = swap_tables(lax.axis_size("clus"), lax.axis_size("sub"))
    return [lax.ppermute(buffer, AXES, table) for buffer, table in zip(buffers, tables)]


def parities():
    even_c = lax.rem(lax.axis_index("clus"), 2) == 0
    even_s = lax.rem(lax.axis_index("sub"), 2) == 0
    return even_c, even_s


def by_swap(values):
    even_c, even_s = parities()
    return [
        jnp.where(even_s, values[1], values[0]),
        jnp.where(even_s, values[0], values[1]),
        jnp.where(even_c, values[2], values[3]),
        jnp.where(even_c, values[3], values[2]),
    ]


def by_direction(values):
    even_c, even_s = parities()
    return [
        jnp.where(even_s, values[1], values[0]),
        jnp.where(even_s, values[0], values[1]),
        jnp.where(even_c, values[2], values[3]),
        jnp.where(even_c, values[3], values[2]),
    ]


def halves(values):
    high = values.astype(BF16)
    return high, (values - high.astype(F32)).astype(BF16)


def product(left, right):
    return jnp.dot(left, right, preferred_element_type=F32)


def full_product(left, right):
    return jnp.dot(left, right, preferred_element_type=F32, precision=FULL)


def full_product_t(left, right):
    return lax.dot_general(left, right, (((1,), (1,)), ((), ())), preferred_element_type=F32, precision=FULL)


def reorder(values, table):
    count = values.shape[0]
    high, rest = halves(values)
    low = (values - high.astype(F32) - rest.astype(F32)).astype(BF16)
    moved = product(jnp.concatenate([high, rest, low]), table)
    return moved[:count] + moved[count:2 * count] + moved[2 * count:]


def times_matrix(values, matrix):
    count = values.shape[0]
    high, low = halves(values)
    both = product(jnp.concatenate([high, low]), matrix)
    return both[:count] + both[count:]


def start_kernel(pair, modes, load, rigid, schur, to_a, to_b, to_c, to_d, diag_out, buffer):
    cases = load.shape[1]
    eye = lax.broadcasted_iota(jnp.int32, (pair, pair), 0) == lax.broadcasted_iota(jnp.int32, (pair, pair), 1)
    buffer[...] = jnp.zeros_like(buffer)
    for d in range(4):
        span = slice(d * pair, (d + 1) * pair)
        diag = jnp.sum(jnp.where(eye, schur[span, span].astype(F32), 0.0), axis=0, keepdims=True)
        diag_out[:, span] = diag
        buffer[d, 0:cases] = load[d]
        buffer[d, cases:cases + modes] = rigid[d]
        buffer[d, cases + STRIP - 1:cases + STRIP] = diag
    for out, values in zip((to_a, to_b, to_c, to_d), by_swap([buffer[d] for d in range(4)])):
        out[...] = values


def gram_kernel(
    pair, modes, devices, load, rigid, schur, diag_own, sign_live, tables, from_a, from_b, from_c, from_d,
    packed, to_a, to_b, to_c, to_d, rhs, first, weight, basis, image, operand, right
):
    cases = load.shape[1]
    span = 3 * STRIP
    arrived = by_direction([from_a[...], from_b[...], from_c[...], from_d[...]])
    basis[...] = jnp.zeros_like(basis)
    right[...] = jnp.zeros_like(right)
    for d in range(4):
        lanes = slice(d * pair, (d + 1) * pair)
        sign = sign_live[:, lanes]
        distant = reorder(arrived[d], tables[d])
        distant_rigid = distant[cases:cases + modes]
        own_rigid = rigid[d]
        both = diag_own[:, lanes] + distant[cases + STRIP - 1:cases + STRIP]
        is_live = sign != 0.0
        inverse = jnp.where(is_live, 1.0 / jnp.where(is_live, both, 1.0), 0.0)
        weight[:, lanes] = inverse
        own_rhs = sign * (load[d] - distant[:cases])
        rhs[:, lanes] = own_rhs
        first[:, lanes] = inverse * own_rhs
        near = own_rigid - distant_rigid if d < 2 else own_rigid
        basis[span + STRIP:span + STRIP + modes, lanes] = sign * near
        if d >= 2:
            at = span if d == 2 else span + 2 * STRIP
            basis[at:at + modes, lanes] = -sign * distant_rigid
        right[6 * modes:7 * modes, lanes] = own_rigid
    basis[0:span] = weight[...] * basis[span:2 * span]
    signs = sign_live[...]
    operand[0:2 * span] = signs * basis[...]
    operand[2 * span:2 * span + cases] = signs * first[...]
    operand[2 * span + cases:2 * span + 2 * cases] = signs * rhs[...]
    image[...] = times_matrix(operand[0:2 * span + cases], schur[...])
    for g in range(6):
        right[g * modes:(g + 1) * modes] = image[g * STRIP:g * STRIP + modes]
    gram = full_product_t(operand[...], right[...])
    lane = lax.broadcasted_iota(jnp.int32, (STRIP, gram.shape[1]), 1)
    strips = []
    for g in range(6):
        strip = gram[g * STRIP:(g + 1) * STRIP]
        own = (lane >= g * modes) & (lane < (g + 1) * modes)
        strips.append(jnp.where(own, 0.5 * strip, strip))
    rows = []
    for row in pack_places(modes):
        total = jnp.zeros_like(strips[0])
        for g, begin, end, at in row:
            piece = strips[g] if at == begin else pltpu.roll(strips[g], (at - begin) % lane.shape[1], 1)
            total = jnp.where((lane >= at) & (lane < at + end - begin), piece, total)
        rows.append(total)
    total = jnp.concatenate(rows)
    lane = lax.broadcasted_iota(jnp.int32, total.shape, 1)
    at = 12 * modes
    with_first = gram[2 * span:2 * span + cases]
    with_rhs = gram[2 * span + cases:2 * span + 2 * cases]
    total = jnp.where(lane >= at, pltpu.roll(with_first, at, 1), total)
    total = jnp.where(lane >= at + 7 * modes, pltpu.roll(with_rhs, at + modes, 1), total)

    def spread(i, carry):
        packed[pl.ds(pl.multiple_of(i * PACK, PACK), PACK)] = total
        return carry

    lax.fori_loop(0, devices, spread, 0, unroll=min(devices, 32))
    parts = [image[:, d * pair:(d + 1) * pair] for d in range(4)]
    for out, values in zip((to_a, to_b, to_c, to_d), by_swap(parts)):
        out[...] = values


def pack_places(modes):
    upper = [(0, 0, 7 * modes, 0), (2, 2 * modes, 7 * modes, 7 * modes)]
    lower = [
        (1, modes, 7 * modes, 0), (3, 3 * modes, 6 * modes, 6 * modes),
        (4, 4 * modes, 6 * modes, 9 * modes), (5, 5 * modes, 6 * modes, 11 * modes),
    ]
    return upper, lower


def basis_kernel(
    pair, clusters, basis, image, sign_live, tables, from_a, from_b, from_c, from_d, stacked, applied_first, wide
):
    span = 3 * STRIP
    rows = 4 * pair
    width = clusters * STRIP
    cluster_at = lax.axis_index("clus")
    arrived = by_direction([from_a[...], from_b[...], from_c[...], from_d[...]])
    wide[...] = jnp.zeros_like(wide)
    near = pl.ds(pl.multiple_of((cluster_at + 1) * STRIP, STRIP), span)
    signs = sign_live[...]
    wide[near, 0:rows] = basis[span:2 * span]
    wide[near, rows:2 * rows] = basis[0:span]
    wide[near, 2 * rows:3 * rows] = signs * image[0:span]
    wide[near, 3 * rows:4 * rows] = signs * image[span:2 * span]
    for d in range(4):
        lanes = slice(d * pair, (d + 1) * pair)
        sign = sign_live[:, lanes]
        distant = sign * reorder(arrived[d], tables[d])
        at = pl.ds(pl.multiple_of((cluster_at + (1, 1, 0, 2)[d]) * STRIP, STRIP), span)
        for k in range(2):
            begin = (2 + k) * rows + d * pair
            wide[at, begin:begin + pair] -= distant[k * span:(k + 1) * span]
        applied_first[:, lanes] = sign * image[2 * span:, lanes] - distant[2 * span:]
    high, low = halves(wide[2 * STRIP:2 * STRIP + width])
    stacked[0:width] = high
    stacked[width:2 * width] = low
    stacked[2 * width:3 * width] = high


def unpack(sums, modes, clusters, cases):
    width = clusters * STRIP
    lane = lax.broadcasted_iota(jnp.int32, (PACK, 128), 1)
    upper, coupling, with_first, tails = {}, {}, {}, {}

    def put(store, key, values, begin, column):
        tile, offset = divmod(column, 128)
        shift = (offset - begin) % 128
        moved = pltpu.roll(values, shift, 1) if shift else values
        mask = lane[:values.shape[0]]
        piece = jnp.where((mask >= offset) & (mask < offset + modes), moved, 0.0)
        key = key + (tile,)
        store[key] = store[key] + piece if key in store else piece

    def group(c, h):
        other = c - 1 + h % 3
        return other, (h // 3) * width + other * STRIP

    for c in range(clusters):
        for half, row in enumerate(pack_places(modes)):
            values = sums[c][half * STRIP:(half + 1) * STRIP]
            for g, begin, end, at in row:
                row_cluster, row_at = group(c, g)
                if not 0 <= row_cluster < clusters:
                    continue
                for h in range(begin // modes, end // modes):
                    source = at + h * modes - begin
                    if h == 6:
                        put(coupling, (row_at // STRIP,), values, source, c * STRIP)
                        continue
                    other, column = group(c, h)
                    if 0 <= other < clusters:
                        put(upper, (row_at // STRIP,), values, source, column)
        for h in range(6):
            other, column = group(c, h)
            if 0 <= other < clusters:
                put(with_first, (), sums[c], 12 * modes + h * modes, column)
        put(tails, (0,), sums[c], 19 * modes, c * STRIP)
        put(tails, (1,), sums[c], 18 * modes, c * STRIP)
    return upper, coupling, with_first, tails


def solve_kernel(
    pair, modes, clusters, subs, cases, gathered, inverse, stacked, rhs, first_part, applied_first, weight, sign_live,
    schur, scalars, to_a, to_b, to_c, to_d, first, applied, second, second_image, upper_ref, couple_ref, row_ref,
    tail_ref
):
    width = clusters * STRIP
    rows = 4 * pair
    sums = []
    for c in range(clusters):
        total = gathered[c * subs * PACK:(c * subs + 1) * PACK]
        for s in range(1, subs):
            total = total + gathered[(c * subs + s) * PACK:(c * subs + s + 1) * PACK]
        sums.append(total)
    upper, coupling, with_first, tails = unpack(sums, modes, clusters, cases)

    def fill(ref, store, height):
        for i in range(ref.shape[0] // height):
            for t in range(ref.shape[1] // 128):
                key = (i, t) if len(next(iter(store))) == 2 else (t,)
                values = store[key] if key in store else jnp.zeros((height, 128), F32)
                ref[i * height:(i + 1) * height, t * 128:(t + 1) * 128] = values

    fill(upper_ref, upper, STRIP)
    fill(couple_ref, coupling, STRIP)
    fill(row_ref, with_first, PACK)
    fill(tail_ref, tails, PACK)

    solver = inverse[...]
    couple_solver = full_product(couple_ref[:, :width], solver)

    def coeffs(straight, weighted):
        both = full_product(jnp.concatenate([straight, weighted]), solver)
        a = both[:PACK]
        return a, both[PACK:] - full_product(a, couple_solver)

    tail = tail_ref[:, :width]
    a_first, b_first = coeffs(tail[:PACK], tail[PACK:])
    c_first = jnp.concatenate([a_first, b_first], axis=1)
    upper_matrix = upper_ref[:, :2 * width]
    parts = row_ref[:, :2 * width] - full_product(c_first, upper_matrix) - full_product_t(c_first, upper_matrix)
    a_second, b_second = coeffs(parts[:, width:], parts[:, :width])

    high, low = halves(jnp.concatenate([a_first, a_second, b_first, b_second]))
    moved = product(jnp.concatenate([high, high, low], axis=1), stacked[...])
    block = [moved[i * PACK:(i + 1) * PACK] for i in range(4)]
    plain, heavy = slice(0, rows), slice(rows, 2 * rows)
    projected = rhs[...] - block[0][:, plain]
    direction = first_part[...] - block[0][:, heavy] - block[2][:, plain]
    image = applied_first[...] - block[0][:, 2 * rows:3 * rows] - block[2][:, 3 * rows:]
    image_projected = image - block[1][:, plain]
    last = weight[...] * image - block[1][:, heavy] - block[3][:, plain]
    first[...] = direction
    applied[...] = image
    second[...] = last
    last_operand = sign_live[...] * last
    last_image = times_matrix(last_operand, schur[...])
    second_image[...] = last_image
    parts = [last_image[:, d * pair:(d + 1) * pair] for d in range(4)]
    for out, values in zip((to_a, to_b, to_c, to_d), by_swap(parts)):
        out[...] = values

    def folded(values):
        return sum(values[:, d * pair:(d + 1) * pair] for d in range(4))

    terms = jnp.concatenate([
        folded(0.5 * (projected * direction)),
        folded(0.5 * (direction * image)),
        folded(0.5 * (projected * last + image_projected * direction)),
        folded(0.5 * (image_projected * last)),
        folded(0.5 * (image * last)),
        folded(last_operand * last_image),
        jnp.zeros((128 - 6 * PACK, pair), F32),
    ])
    row = full_product_t(jnp.ones((STRIP, pair), F32), terms)[0:1]
    scalars[...] = jnp.broadcast_to(row[:, None, :], scalars.shape)


def far_kernel(pair, image, sign_live, tables, from_a, from_b, from_c, from_d, applied):
    arrived = by_direction([from_a[...], from_b[...], from_c[...], from_d[...]])
    for d in range(4):
        lanes = slice(d * pair, (d + 1) * pair)
        applied[:, lanes] = sign_live[:, lanes] * (image[:, lanes] - reorder(arrived[d], tables[d]))


def end_kernel(pair, scalars, rhs, first, applied, second, second_applied, multipliers, residual):
    total = jnp.sum(scalars[...], axis=0)
    rho_one, delta_one, cross, square, mixed, delta_last = [
        total if i == 0 else pltpu.roll(total, 128 - i * PACK, 1) for i in range(6)
    ]
    alpha_one = rho_one / delta_one
    rho_two = rho_one - alpha_one * cross + alpha_one * alpha_one * square
    grow = 1.0 + rho_two / rho_one
    delta_two = grow * grow * delta_one - 2.0 * grow * alpha_one * mixed + alpha_one * alpha_one * delta_last
    alpha_two = rho_two / delta_two
    eye = lax.broadcasted_iota(jnp.int32, (PACK, 128), 0) == lax.broadcasted_iota(jnp.int32, (PACK, 128), 1)

    def column(values):
        return jnp.sum(jnp.where(eye, values, 0.0), axis=1, keepdims=True)

    keep = column(alpha_one + alpha_two * grow)
    drop = column(alpha_two * alpha_one)
    new_multipliers = keep * first[...] - drop * second[...]
    new_residual = rhs[...] - keep * applied[...] + drop * second_applied[...]
    for d in range(4):
        lanes = slice(d * pair, (d + 1) * pair)
        multipliers[d] = new_multipliers[:, lanes]
        residual[d] = new_residual[:, lanes]


def call(kernel, outs, scratch, *args):
    return pl.pallas_call(
        kernel,
        out_shape=[jax.ShapeDtypeStruct(shape, dtype) for shape, dtype in outs],
        in_specs=[pl.BlockSpec(memory_space=pltpu.VMEM)] * len(args),
        out_specs=[pl.BlockSpec(memory_space=pltpu.VMEM)] * len(outs),
        scratch_shapes=[pltpu.VMEM(shape, dtype) for shape, dtype in scratch],
        compiler_params=pltpu.CompilerParams(vmem_limit_bytes=VMEM_LIMIT),
    )(*args)


def shards(schur, load, rigid, lengths, partner, coarse_inverse):
    own_load, own_rigid, matrix = load[0, 0], rigid[0, 0], schur[0, 0]
    cases, pair = own_load.shape[1:]
    modes = own_rigid.shape[1]
    clusters, subs = lax.axis_size("clus"), lax.axis_size("sub")
    devices = clusters * subs
    rows = 4 * pair
    width = clusters * STRIP
    lanes = max(width, 128)
    span = 3 * STRIP

    tables = (partner[0, 0][:, None, :] == lax.broadcasted_iota(jnp.int32, (4, pair, pair), 1)).astype(BF16)
    live = lax.broadcasted_iota(jnp.int32, (4, pair), 1) < lengths[0, 0][:, None]
    sign = jnp.array([-1.0, 1.0, -1.0, 1.0], F32)[:, None]
    sign_live = jnp.where(live, sign, 0.0).reshape(1, rows)
    wide_inverse = jnp.pad(
        coarse_inverse.reshape(clusters, modes, clusters, modes),
        ((0, 0), (0, STRIP - modes), (0, 0), (0, STRIP - modes)),
    ).reshape(width, width)

    flat = ((cases, rows), F32)
    *sent, diag_own = call(
        functools.partial(start_kernel, pair, modes),
        [((cases + STRIP, pair), F32)] * 4 + [((1, rows), F32)],
        [((4, cases + STRIP, pair), F32)],
        own_load, own_rigid, matrix,
    )
    arrived = swap(sent)

    packed, *sent, rhs, first_part, weight, basis, image = call(
        functools.partial(gram_kernel, pair, modes, devices),
        [((devices * PACK, 128), F32)] + [((2 * span + cases, pair), F32)] * 4
        + [flat, flat, ((1, rows), F32), ((2 * span, rows), F32), ((2 * span + cases, rows), F32)],
        [((2 * span + 2 * cases, rows), F32), ((128, rows), F32)],
        own_load, own_rigid, matrix, diag_own, sign_live, tables, *arrived,
    )
    gathered = lax.all_to_all(packed, AXES, 0, 0, tiled=True)
    arrived = swap(sent)
    stacked, applied_first = call(
        functools.partial(basis_kernel, pair, clusters),
        [((3 * width, 4 * rows), BF16), flat],
        [((width + 4 * STRIP, 4 * rows), F32)],
        basis, image, sign_live, tables, *arrived,
    )

    scalars, *sent, first, applied, second, second_image = call(
        functools.partial(solve_kernel, pair, modes, clusters, subs, cases),
        [((devices, 1, 128), F32)] + [((cases, pair), F32)] * 4 + [flat] * 4,
        [((2 * width, max(2 * width, 128)), F32), ((width, lanes), F32), ((PACK, max(2 * width, 128)), F32),
         ((2 * PACK, lanes), F32)],
        gathered, wide_inverse, stacked, rhs, first_part, applied_first, weight, sign_live, matrix,
    )
    gathered = lax.all_to_all(scalars, AXES, 0, 0, tiled=True)
    arrived = swap(sent)
    (second_applied,) = call(
        functools.partial(far_kernel, pair), [flat], [], second_image, sign_live, tables, *arrived
    )
    multipliers, residual = call(
        functools.partial(end_kernel, pair), [((4, cases, pair), F32)] * 2, [],
        gathered, rhs, first, applied, second, second_applied,
    )
    return (multipliers[None, None], residual[None, None])


def solution(mesh):
    in_specs = (
        P("clus", "sub", None, None),
        P("clus", "sub", None, None, None),
        P("clus", "sub", None, None, None),
        P("clus", "sub", None),
        P("clus", "sub", None, None),
        P(),
    )
    out_specs = (P("clus", "sub", None, None, None), P("clus", "sub", None, None, None))
    return jax.shard_map(shards, mesh=mesh, in_specs=in_specs, out_specs=out_specs, check_vma=False)
```

```python
import functools

import jax
import jax.numpy as jnp
from jax import lax
from jax.experimental import pallas as pl
from jax.experimental.pallas import tpu as pltpu
from jax.sharding import PartitionSpec as P

AXES = ("clus", "sub")
F32 = jnp.float32
BF16 = jnp.bfloat16
FULL = lax.Precision.HIGHEST
STRIP = 8
PACK = 16
VMEM_LIMIT = 48 * 1024 * 1024


def pair_even(index, count):
    other = index ^ 1
    return other if other < count else index


def pair_odd(index, count):
    other = ((index - 1) ^ 1) + 1
    return other if index > 0 and other < count else index


def swap_tables(clusters, subs):
    sub_even, sub_odd, clus_odd, clus_even = [], [], [], []
    for c in range(clusters):
        for s in range(subs):
            here = c * subs + s
            sub_even.append((here, c * subs + pair_even(s, subs)))
            odd = pair_odd(s, subs)
            target = c * subs + odd if odd != s else pair_even(c, clusters) * subs + s
            sub_odd.append((here, target))
            odd = pair_odd(c, clusters)
            target = odd * subs + s if odd != c else c * subs + pair_even(s, subs)
            clus_odd.append((here, target))
            clus_even.append((here, pair_even(c, clusters) * subs + s))
    return sub_even, sub_odd, clus_odd, clus_even


def swap(buffers):
    tables = swap_tables(lax.axis_size("clus"), lax.axis_size("sub"))
    return [lax.ppermute(buffer, AXES, table) for buffer, table in zip(buffers, tables)]


def parities():
    even_c = lax.rem(lax.axis_index("clus"), 2) == 0
    even_s = lax.rem(lax.axis_index("sub"), 2) == 0
    return even_c, even_s


def by_swap(values):
    even_c, even_s = parities()
    return [
        jnp.where(even_s, values[1], values[0]),
        jnp.where(even_s, values[0], values[1]),
        jnp.where(even_c, values[2], values[3]),
        jnp.where(even_c, values[3], values[2]),
    ]


def by_direction(values):
    even_c, even_s = parities()
    return [
        jnp.where(even_s, values[1], values[0]),
        jnp.where(even_s, values[0], values[1]),
        jnp.where(even_c, values[2], values[3]),
        jnp.where(even_c, values[3], values[2]),
    ]


def halves(values):
    high = values.astype(BF16)
    return high, (values - high.astype(F32)).astype(BF16)


def product(left, right):
    return jnp.dot(left, right, preferred_element_type=F32)


def full_product(left, right):
    return jnp.dot(left, right, preferred_element_type=F32, precision=FULL)


def full_product_t(left, right):
    return lax.dot_general(left, right, (((1,), (1,)), ((), ())), preferred_element_type=F32, precision=FULL)


def reorder(values, table):
    count = values.shape[0]
    high, rest = halves(values)
    low = (values - high.astype(F32) - rest.astype(F32)).astype(BF16)
    moved = product(jnp.concatenate([high, rest, low]), table)
    return moved[:count] + moved[count:2 * count] + moved[2 * count:]


def times_matrix(values, matrix):
    count = values.shape[0]
    high, low = halves(values)
    both = product(jnp.concatenate([high, low]), matrix)
    return both[:count] + both[count:]


def start_kernel(
    pair, modes, load_hbm, rigid_hbm, schur_hbm, to_a, to_b, to_c, to_d, diag_out, load, rigid, buffer, blocks, arrivals
):
    cases = load.shape[1]
    copies = [
        pltpu.make_async_copy(load_hbm, load, arrivals.at[0]),
        pltpu.make_async_copy(rigid_hbm, rigid, arrivals.at[1]),
    ]
    for d in range(4):
        span = slice(d * pair, (d + 1) * pair)
        copies.append(pltpu.make_async_copy(schur_hbm.at[span, span], blocks.at[d], arrivals.at[2 + d]))
    for copy in copies:
        copy.start()
    eye = lax.broadcasted_iota(jnp.int32, (pair, pair), 0) == lax.broadcasted_iota(jnp.int32, (pair, pair), 1)
    buffer[...] = jnp.zeros_like(buffer)
    for copy in copies:
        copy.wait()
    for d in range(4):
        span = slice(d * pair, (d + 1) * pair)
        diag = jnp.sum(jnp.where(eye, blocks[d].astype(F32), 0.0), axis=0, keepdims=True)
        diag_out[:, span] = diag
        buffer[d, 0:cases] = load[d]
        buffer[d, cases:cases + modes] = rigid[:, d]
        buffer[d, cases + STRIP - 1:cases + STRIP] = diag
    for out, values in zip((to_a, to_b, to_c, to_d), by_swap([buffer[d] for d in range(4)])):
        out[...] = values


def gram_kernel(
    pair, modes, clusters, subs, load, rigid, schur, diag_own, sign_live, tables, from_a, from_b, from_c, from_d,
    packed, to_a, to_b, to_c, to_d, rhs, first, weight, basis, image, operand, right
):
    cases = load.shape[1]
    span = 3 * STRIP
    arrived = by_direction([from_a[...], from_b[...], from_c[...], from_d[...]])
    basis[...] = jnp.zeros_like(basis)
    right[...] = jnp.zeros_like(right)
    for d in range(4):
        lanes = slice(d * pair, (d + 1) * pair)
        sign = sign_live[:, lanes]
        distant = reorder(arrived[d], tables[d])
        distant_rigid = distant[cases:cases + modes]
        own_rigid = rigid[:, d]
        both = diag_own[:, lanes] + distant[cases + STRIP - 1:cases + STRIP]
        is_live = sign != 0.0
        inverse = jnp.where(is_live, 1.0 / jnp.where(is_live, both, 1.0), 0.0)
        weight[:, lanes] = inverse
        own_rhs = sign * (load[d] - distant[:cases])
        rhs[:, lanes] = own_rhs
        first[:, lanes] = inverse * own_rhs
        near = own_rigid - distant_rigid if d < 2 else own_rigid
        basis[span + STRIP:span + STRIP + modes, lanes] = sign * near
        if d >= 2:
            at = span if d == 2 else span + 2 * STRIP
            basis[at:at + modes, lanes] = -sign * distant_rigid
        right[6 * modes:7 * modes, lanes] = own_rigid
    basis[0:span] = weight[...] * basis[span:2 * span]
    signs = sign_live[...]
    operand[0:2 * span] = signs * basis[...]
    operand[2 * span:2 * span + cases] = signs * first[...]
    operand[2 * span + cases:2 * span + 2 * cases] = signs * rhs[...]
    image[...] = times_matrix(operand[0:2 * span + cases], schur[...])
    for g in range(6):
        right[g * modes:(g + 1) * modes] = image[g * STRIP:g * STRIP + modes]
    gram = full_product_t(operand[...], right[...])
    lane = lax.broadcasted_iota(jnp.int32, (STRIP, gram.shape[1]), 1)
    strips = []
    for g in range(6):
        strip = gram[g * STRIP:(g + 1) * STRIP]
        own = (lane >= g * modes) & (lane < (g + 1) * modes)
        strips.append(jnp.where(own, 0.5 * strip, strip))
    rows = []
    for row in pack_places(modes):
        total = jnp.zeros_like(strips[0])
        for g, begin, end, at in row:
            piece = strips[g] if at == begin else pltpu.roll(strips[g], (at - begin) % lane.shape[1], 1)
            total = jnp.where((lane >= at) & (lane < at + end - begin), piece, total)
        rows.append(total)
    total = jnp.concatenate(rows)
    lane = lax.broadcasted_iota(jnp.int32, total.shape, 1)
    at = 12 * modes
    with_first = gram[2 * span:2 * span + cases]
    with_rhs = gram[2 * span + cases:2 * span + 2 * cases]
    total = jnp.where(lane >= at, pltpu.roll(with_first, at, 1), total)
    total = jnp.where(lane >= at + 7 * modes, pltpu.roll(with_rhs, at + modes, 1), total)

    halves_out = [jnp.concatenate([total[h * STRIP:(h + 1) * STRIP]] * subs) for h in range(2)]
    for c in range(clusters):
        packed[c * subs * STRIP:(c + 1) * subs * STRIP] = halves_out[c % 2]
    parts = [image[:, d * pair:(d + 1) * pair] for d in range(4)]
    for out, values in zip((to_a, to_b, to_c, to_d), by_swap(parts)):
        out[...] = values


def pack_places(modes):
    upper = [(0, 0, 7 * modes, 0), (2, 2 * modes, 7 * modes, 7 * modes)]
    lower = [
        (1, modes, 7 * modes, 0), (3, 3 * modes, 6 * modes, 6 * modes),
        (4, 4 * modes, 6 * modes, 9 * modes), (5, 5 * modes, 6 * modes, 11 * modes),
    ]
    return upper, lower


def basis_kernel(
    pair, clusters, basis, image, sign_live, tables, from_a, from_b, from_c, from_d, stacked, applied_first, wide
):
    span = 3 * STRIP
    rows = 4 * pair
    width = clusters * STRIP
    cluster_at = lax.axis_index("clus")
    arrived = by_direction([from_a[...], from_b[...], from_c[...], from_d[...]])
    wide[...] = jnp.zeros_like(wide)
    near = pl.ds(pl.multiple_of((cluster_at + 1) * STRIP, STRIP), span)
    signs = sign_live[...]
    wide[near, 0:rows] = basis[span:2 * span]
    wide[near, rows:2 * rows] = basis[0:span]
    wide[near, 2 * rows:3 * rows] = signs * image[0:span]
    wide[near, 3 * rows:4 * rows] = signs * image[span:2 * span]
    for d in range(4):
        lanes = slice(d * pair, (d + 1) * pair)
        sign = sign_live[:, lanes]
        distant = sign * reorder(arrived[d], tables[d])
        at = pl.ds(pl.multiple_of((cluster_at + (1, 1, 0, 2)[d]) * STRIP, STRIP), span)
        for k in range(2):
            begin = (2 + k) * rows + d * pair
            wide[at, begin:begin + pair] -= distant[k * span:(k + 1) * span]
        applied_first[:, lanes] = sign * image[2 * span:, lanes] - distant[2 * span:]
    high, low = halves(wide[2 * STRIP:2 * STRIP + width])
    stacked[0:width] = high
    stacked[width:2 * width] = low
    stacked[2 * width:3 * width] = high


def unpack(strips, modes, clusters):
    width = clusters * STRIP
    lane = lax.broadcasted_iota(jnp.int32, (PACK, 128), 1)
    upper, coupling, with_first, tails = {}, {}, {}, {}

    def put(store, key, values, begin, column):
        tile, offset = divmod(column, 128)
        shift = (offset - begin) % 128
        moved = pltpu.roll(values, shift, 1) if shift else values
        mask = lane[:values.shape[0]]
        piece = jnp.where((mask >= offset) & (mask < offset + modes), moved, 0.0)
        key = key + (tile,)
        store[key] = store[key] + piece if key in store else piece

    def group(c, h):
        other = c - 1 + h % 3
        return other, (h // 3) * width + other * STRIP

    for c in range(clusters):
        whole = jnp.concatenate(strips[c])
        for half, row in enumerate(pack_places(modes)):
            values = strips[c][half]
            for g, begin, end, at in row:
                row_cluster, row_at = group(c, g)
                if not 0 <= row_cluster < clusters:
                    continue
                for h in range(begin // modes, end // modes):
                    source = at + h * modes - begin
                    if h == 6:
                        put(coupling, (row_at // STRIP,), values, source, c * STRIP)
                        continue
                    other, column = group(c, h)
                    if 0 <= other < clusters:
                        put(upper, (row_at // STRIP,), values, source, column)
        for h in range(6):
            other, column = group(c, h)
            if 0 <= other < clusters:
                put(with_first, (), whole, 12 * modes + h * modes, column)
        put(tails, (0,), whole, 19 * modes, c * STRIP)
        put(tails, (1,), whole, 18 * modes, c * STRIP)
    return upper, coupling, with_first, tails


def solve_kernel(
    pair, modes, clusters, mine, other, inverse, stacked, rhs, first_part, applied_first, weight, sign_live,
    schur, scalars, to_a, to_b, to_c, to_d, first, applied, second, second_image, upper_ref, couple_ref, row_ref,
    tail_ref
):
    width = clusters * STRIP
    rows = 4 * pair
    even_c, _ = parities()
    strips = []
    for c in range(clusters):
        span = slice(c * STRIP, (c + 1) * STRIP)
        strips.append((jnp.where(even_c, mine[span], other[span]), jnp.where(even_c, other[span], mine[span])))
    upper, coupling, with_first, tails = unpack(strips, modes, clusters)

    def fill(ref, store, height):
        for i in range(ref.shape[0] // height):
            for t in range(ref.shape[1] // 128):
                key = (i, t) if len(next(iter(store))) == 2 else (t,)
                values = store[key] if key in store else jnp.zeros((height, 128), F32)
                ref[i * height:(i + 1) * height, t * 128:(t + 1) * 128] = values

    fill(upper_ref, upper, STRIP)
    fill(couple_ref, coupling, STRIP)
    fill(row_ref, with_first, PACK)
    fill(tail_ref, tails, PACK)

    solver = inverse[...]
    couple_solver = full_product(couple_ref[:, :width], solver)

    def coeffs(straight, weighted):
        both = full_product(jnp.concatenate([straight, weighted]), solver)
        a = both[:PACK]
        return a, both[PACK:] - full_product(a, couple_solver)

    tail = tail_ref[:, :width]
    a_first, b_first = coeffs(tail[:PACK], tail[PACK:])
    c_first = jnp.concatenate([a_first, b_first], axis=1)
    upper_matrix = upper_ref[:, :2 * width]
    parts = row_ref[:, :2 * width] - full_product(c_first, upper_matrix) - full_product_t(c_first, upper_matrix)
    a_second, b_second = coeffs(parts[:, width:], parts[:, :width])

    high, low = halves(jnp.concatenate([a_first, a_second, b_first, b_second]))
    moved = product(jnp.concatenate([high, high, low], axis=1), stacked[...])
    block = [moved[i * PACK:(i + 1) * PACK] for i in range(4)]
    plain, heavy = slice(0, rows), slice(rows, 2 * rows)
    projected = rhs[...] - block[0][:, plain]
    direction = first_part[...] - block[0][:, heavy] - block[2][:, plain]
    image = applied_first[...] - block[0][:, 2 * rows:3 * rows] - block[2][:, 3 * rows:]
    image_projected = image - block[1][:, plain]
    last = weight[...] * image - block[1][:, heavy] - block[3][:, plain]
    first[...] = direction
    applied[...] = image
    second[...] = last
    last_operand = sign_live[...] * last
    last_image = times_matrix(last_operand, schur[...])
    second_image[...] = last_image
    parts = [last_image[:, d * pair:(d + 1) * pair] for d in range(4)]
    for out, values in zip((to_a, to_b, to_c, to_d), by_swap(parts)):
        out[...] = values

    def folded(values):
        return sum(values[:, d * pair:(d + 1) * pair] for d in range(4))

    terms = jnp.concatenate([
        folded(0.5 * (projected * direction)),
        folded(0.5 * (direction * image)),
        folded(0.5 * (projected * last + image_projected * direction)),
        folded(0.5 * (image_projected * last)),
        folded(0.5 * (image * last)),
        folded(last_operand * last_image),
        jnp.zeros((128 - 6 * PACK, pair), F32),
    ])
    row = full_product_t(jnp.ones((STRIP, pair), F32), terms)[0:1]
    scalars[...] = jnp.broadcast_to(row[:, None, :], scalars.shape)


def far_kernel(pair, image, sign_live, tables, from_a, from_b, from_c, from_d, applied):
    arrived = by_direction([from_a[...], from_b[...], from_c[...], from_d[...]])
    for d in range(4):
        lanes = slice(d * pair, (d + 1) * pair)
        applied[:, lanes] = sign_live[:, lanes] * (image[:, lanes] - reorder(arrived[d], tables[d]))


def end_kernel(pair, scalars, rhs, first, applied, second, second_applied, multipliers, residual):
    total = jnp.sum(scalars[...], axis=0)
    rho_one, delta_one, cross, square, mixed, delta_last = [
        total if i == 0 else pltpu.roll(total, 128 - i * PACK, 1) for i in range(6)
    ]
    alpha_one = rho_one / delta_one
    rho_two = rho_one - alpha_one * cross + alpha_one * alpha_one * square
    grow = 1.0 + rho_two / rho_one
    delta_two = grow * grow * delta_one - 2.0 * grow * alpha_one * mixed + alpha_one * alpha_one * delta_last
    alpha_two = rho_two / delta_two
    eye = lax.broadcasted_iota(jnp.int32, (PACK, 128), 0) == lax.broadcasted_iota(jnp.int32, (PACK, 128), 1)

    def column(values):
        return jnp.sum(jnp.where(eye, values, 0.0), axis=1, keepdims=True)

    keep = column(alpha_one + alpha_two * grow)
    drop = column(alpha_two * alpha_one)
    new_multipliers = keep * first[...] - drop * second[...]
    new_residual = rhs[...] - keep * applied[...] + drop * second_applied[...]
    for d in range(4):
        lanes = slice(d * pair, (d + 1) * pair)
        multipliers[d] = new_multipliers[:, lanes]
        residual[d] = new_residual[:, lanes]


def call(kernel, outs, scratch, *args, place=pltpu.VMEM):
    return pl.pallas_call(
        kernel,
        out_shape=[jax.ShapeDtypeStruct(shape, dtype) for shape, dtype in outs],
        in_specs=[pl.BlockSpec(memory_space=place)] * len(args),
        out_specs=[pl.BlockSpec(memory_space=pltpu.VMEM)] * len(outs),
        scratch_shapes=scratch,
        compiler_params=pltpu.CompilerParams(vmem_limit_bytes=VMEM_LIMIT),
    )(*args)


def shards(schur, load, rigid, lengths, partner, coarse_inverse):
    own_load, matrix = load[0, 0], schur[0, 0]
    own_rigid = jnp.swapaxes(rigid[0, 0], 0, 1)
    cases, pair = own_load.shape[1:]
    modes = own_rigid.shape[0]
    clusters, subs = lax.axis_size("clus"), lax.axis_size("sub")
    devices = clusters * subs
    rows = 4 * pair
    width = clusters * STRIP
    lanes = max(width, 128)
    span = 3 * STRIP

    tables = (partner[0, 0][:, None, :] == lax.broadcasted_iota(jnp.int32, (4, pair, pair), 1)).astype(BF16)
    live = lax.broadcasted_iota(jnp.int32, (4, pair), 1) < lengths[0, 0][:, None]
    sign = jnp.array([-1.0, 1.0, -1.0, 1.0], F32)[:, None]
    sign_live = jnp.where(live, sign, 0.0).reshape(1, rows)
    wide_inverse = jnp.pad(
        coarse_inverse.reshape(clusters, modes, clusters, modes),
        ((0, 0), (0, STRIP - modes), (0, 0), (0, STRIP - modes)),
    ).reshape(width, width)

    flat = ((cases, rows), F32)
    *sent, diag_own, own_load, own_rigid = call(
        functools.partial(start_kernel, pair, modes),
        [((cases + STRIP, pair), F32)] * 4 + [((1, rows), F32), (own_load.shape, F32), (own_rigid.shape, F32)],
        [pltpu.VMEM((4, cases + STRIP, pair), F32), pltpu.VMEM((4, pair, pair), BF16), pltpu.SemaphoreType.DMA((6,))],
        own_load, own_rigid, matrix, place=pltpu.HBM,
    )
    arrived = swap(sent)

    packed, *sent, rhs, first_part, weight, basis, image = call(
        functools.partial(gram_kernel, pair, modes, clusters, subs),
        [((devices * STRIP, 128), F32)] + [((2 * span + cases, pair), F32)] * 4
        + [flat, flat, ((1, rows), F32), ((2 * span, rows), F32), ((2 * span + cases, rows), F32)],
        [pltpu.VMEM((2 * span + 2 * cases, rows), F32), pltpu.VMEM((128, rows), F32)],
        own_load, own_rigid, matrix, diag_own, sign_live, tables, *arrived,
    )
    gathered = lax.all_to_all(packed, AXES, 0, 0, tiled=True)
    arrived = swap(sent)
    stacked, applied_first = call(
        functools.partial(basis_kernel, pair, clusters),
        [((3 * width, 4 * rows), BF16), flat],
        [pltpu.VMEM((width + 4 * STRIP, 4 * rows), F32)],
        basis, image, sign_live, tables, *arrived,
    )

    mine = jnp.sum(gathered.reshape(clusters, subs, STRIP, 128), axis=1).reshape(width, 128)
    other = lax.ppermute(mine, AXES, swap_tables(clusters, subs)[3])
    scalars, *sent, first, applied, second, second_image = call(
        functools.partial(solve_kernel, pair, modes, clusters),
        [((devices, 1, 128), F32)] + [((cases, pair), F32)] * 4 + [flat] * 4,
        [pltpu.VMEM(shape, F32) for shape in
         ((2 * width, max(2 * width, 128)), (width, lanes), (PACK, max(2 * width, 128)), (2 * PACK, lanes))],
        mine, other, wide_inverse, stacked, rhs, first_part, applied_first, weight, sign_live, matrix,
    )
    gathered = lax.all_to_all(scalars, AXES, 0, 0, tiled=True)
    arrived = swap(sent)
    (second_applied,) = call(
        functools.partial(far_kernel, pair), [flat], [], second_image, sign_live, tables, *arrived
    )
    multipliers, residual = call(
        functools.partial(end_kernel, pair), [((4, cases, pair), F32)] * 2, [],
        gathered, rhs, first, applied, second, second_applied,
    )
    return (multipliers[None, None], residual[None, None])


def solution(mesh):
    in_specs = (
        P("clus", "sub", None, None),
        P("clus", "sub", None, None, None),
        P("clus", "sub", None, None, None),
        P("clus", "sub", None),
        P("clus", "sub", None, None),
        P(),
    )
    out_specs = (P("clus", "sub", None, None, None), P("clus", "sub", None, None, None))
    return jax.shard_map(shards, mesh=mesh, in_specs=in_specs, out_specs=out_specs, check_vma=False)
```

```python
import functools

import jax
import jax.numpy as jnp
from jax import lax
from jax.experimental import pallas as pl
from jax.experimental.pallas import tpu as pltpu
from jax.sharding import PartitionSpec as P

AXES = ("clus", "sub")
F32 = jnp.float32
BF16 = jnp.bfloat16
FULL = lax.Precision.HIGHEST
STRIP = 8
PACK = 16
MIB = 1024 * 1024


def pair_even(index, count):
    other = index ^ 1
    return other if other < count else index


def pair_odd(index, count):
    other = ((index - 1) ^ 1) + 1
    return other if index > 0 and other < count else index


def swap_tables(clusters, subs):
    sub_even, sub_odd, clus_odd, clus_even = [], [], [], []
    for c in range(clusters):
        for s in range(subs):
            here = c * subs + s
            sub_even.append((here, c * subs + pair_even(s, subs)))
            odd = pair_odd(s, subs)
            target = c * subs + odd if odd != s else pair_even(c, clusters) * subs + s
            sub_odd.append((here, target))
            odd = pair_odd(c, clusters)
            target = odd * subs + s if odd != c else c * subs + pair_even(s, subs)
            clus_odd.append((here, target))
            clus_even.append((here, pair_even(c, clusters) * subs + s))
    return sub_even, sub_odd, clus_odd, clus_even


def swap(buffers):
    tables = swap_tables(lax.axis_size("clus"), lax.axis_size("sub"))
    return [lax.ppermute(buffer, AXES, table) for buffer, table in zip(buffers, tables)]


def parities():
    even_c = lax.rem(lax.axis_index("clus"), 2) == 0
    even_s = lax.rem(lax.axis_index("sub"), 2) == 0
    return even_c, even_s


def by_swap(values):
    even_c, even_s = parities()
    return [
        jnp.where(even_s, values[1], values[0]),
        jnp.where(even_s, values[0], values[1]),
        jnp.where(even_c, values[2], values[3]),
        jnp.where(even_c, values[3], values[2]),
    ]


def by_direction(values):
    even_c, even_s = parities()
    return [
        jnp.where(even_s, values[1], values[0]),
        jnp.where(even_s, values[0], values[1]),
        jnp.where(even_c, values[2], values[3]),
        jnp.where(even_c, values[3], values[2]),
    ]


def halves(values):
    high = values.astype(BF16)
    return high, (values - high.astype(F32)).astype(BF16)


def product(left, right):
    return jnp.dot(left, right, preferred_element_type=F32)


def full_product(left, right):
    return jnp.dot(left, right, preferred_element_type=F32, precision=FULL)


def full_product_t(left, right):
    return lax.dot_general(left, right, (((1,), (1,)), ((), ())), preferred_element_type=F32, precision=FULL)


def reorder(values, table):
    count = values.shape[0]
    high, rest = halves(values)
    low = (values - high.astype(F32) - rest.astype(F32)).astype(BF16)
    moved = product(jnp.concatenate([high, rest, low]), table)
    return moved[:count] + moved[count:2 * count] + moved[2 * count:]


def times_matrix(values, matrix):
    count = values.shape[0]
    high, low = halves(values)
    both = product(jnp.concatenate([high, low]), matrix)
    return both[:count] + both[count:]


def start_kernel(
    pair, modes, load_hbm, rigid_hbm, schur_hbm, to_a, to_b, to_c, to_d, load, rigid, buffer, blocks, arrivals
):
    cases = load.shape[1]
    copies = [
        pltpu.make_async_copy(load_hbm, load, arrivals.at[0]),
        pltpu.make_async_copy(rigid_hbm, rigid, arrivals.at[1]),
    ]
    for d in range(4):
        span = slice(d * pair, (d + 1) * pair)
        copies.append(pltpu.make_async_copy(schur_hbm.at[span, span], blocks.at[d], arrivals.at[2 + d]))
    for copy in copies:
        copy.start()
    eye = lax.broadcasted_iota(jnp.int32, (pair, pair), 0) == lax.broadcasted_iota(jnp.int32, (pair, pair), 1)
    buffer[...] = jnp.zeros_like(buffer)
    for copy in copies:
        copy.wait()
    for d in range(4):
        buffer[d, 0:cases] = load[d]
        buffer[d, cases:cases + modes] = rigid[:, d]
        buffer[d, cases + STRIP - 1:cases + STRIP] = jnp.sum(
            jnp.where(eye, blocks[d].astype(F32), 0.0), axis=0, keepdims=True
        )
    for out, values in zip((to_a, to_b, to_c, to_d), by_swap([buffer[d] for d in range(4)])):
        out[...] = values


def fetch_kernel(pair, schur_hbm, partner_hbm, lengths_hbm, schur, tables, sign_live, partner, lengths, arrivals):
    copies = [
        pltpu.make_async_copy(partner_hbm, partner, arrivals.at[0]),
        pltpu.make_async_copy(lengths_hbm, lengths, arrivals.at[1]),
        pltpu.make_async_copy(schur_hbm, schur, arrivals.at[2]),
    ]
    for copy in copies:
        copy.start()
    row = lax.broadcasted_iota(jnp.int32, (pair, pair), 0)
    lane = lax.broadcasted_iota(jnp.int32, (1, pair), 1)
    copies[0].wait()
    copies[1].wait()
    for d in range(4):
        tables[d] = jnp.where(partner[d:d + 1] == row, 1.0, 0.0).astype(BF16)
        sign_live[:, d * pair:(d + 1) * pair] = jnp.where(lane < lengths[:, d:d + 1], (-1.0, 1.0)[d % 2], 0.0)
    copies[2].wait()


def gram_kernel(
    pair, modes, clusters, subs, cases, schur, sign_live, tables, sent_a, sent_b, sent_c, sent_d, from_a, from_b,
    from_c, from_d, packed, to_a, to_b, to_c, to_d, rhs, first, weight, basis, image, operand, right, copies, ready
):
    span = 3 * STRIP
    own = by_direction([sent_a[...], sent_b[...], sent_c[...], sent_d[...]])
    arrived = by_direction([from_a[...], from_b[...], from_c[...], from_d[...]])
    distant = [reorder(arrived[d], tables[d]) for d in range(4)]
    is_mode = lax.broadcasted_iota(jnp.int32, (STRIP, pair), 0) < modes
    none = jnp.zeros((STRIP, pair), F32)
    right[...] = jnp.zeros_like(right)
    for d in range(4):
        lanes = slice(d * pair, (d + 1) * pair)
        sign = sign_live[:, lanes]
        own_tile, far_tile = own[d][cases:], distant[d][cases:]
        both = own_tile[STRIP - 1:] + far_tile[STRIP - 1:]
        is_live = sign != 0.0
        inverse = jnp.where(is_live, 1.0 / jnp.where(is_live, both, 1.0), 0.0)
        weight[:, lanes] = inverse
        own_rhs = sign * (own[d][:cases] - distant[d][:cases])
        own_first = inverse * own_rhs
        rhs[:, lanes] = own_rhs
        first[:, lanes] = own_first
        operand[2 * span:2 * span + cases, lanes] = sign * own_first
        operand[2 * span + cases:2 * span + 2 * cases, lanes] = sign * own_rhs
        near = jnp.where(is_mode, own_tile - far_tile if d < 2 else own_tile, 0.0) * sign
        far = jnp.where(is_mode, -far_tile, 0.0) * sign
        for slot, values in enumerate((far if d == 2 else none, near, far if d == 3 else none)):
            heavy = slice(slot * STRIP, (slot + 1) * STRIP)
            plain = slice(span + slot * STRIP, span + (slot + 1) * STRIP)
            basis[heavy, lanes] = inverse * values
            basis[plain, lanes] = values
            operand[heavy, lanes] = sign * (inverse * values)
            operand[plain, lanes] = sign * values
        right[6 * modes:7 * modes, lanes] = own_tile[:modes]
    image[...] = times_matrix(operand[0:2 * span + cases], schur[...])
    for g in range(6):
        right[g * modes:(g + 1) * modes] = image[g * STRIP:g * STRIP + modes]
    gram = full_product_t(operand[...], right[...])
    lane = lax.broadcasted_iota(jnp.int32, (STRIP, gram.shape[1]), 1)
    strips = []
    for g in range(6):
        strip = gram[g * STRIP:(g + 1) * STRIP]
        own = (lane >= g * modes) & (lane < (g + 1) * modes)
        strips.append(jnp.where(own, 0.5 * strip, strip))
    rows = []
    for row in pack_places(modes):
        total = jnp.zeros_like(strips[0])
        for g, begin, end, at in row:
            piece = strips[g] if at == begin else pltpu.roll(strips[g], (at - begin) % lane.shape[1], 1)
            total = jnp.where((lane >= at) & (lane < at + end - begin), piece, total)
        rows.append(total)
    total = jnp.concatenate(rows)
    lane = lax.broadcasted_iota(jnp.int32, total.shape, 1)
    at = 12 * modes
    with_first = gram[2 * span:2 * span + cases]
    with_rhs = gram[2 * span + cases:2 * span + 2 * cases]
    total = jnp.where(lane >= at, pltpu.roll(with_first, at, 1), total)
    total = jnp.where(lane >= at + 7 * modes, pltpu.roll(with_rhs, at + modes, 1), total)

    strips = [jnp.concatenate([total[h * STRIP:(h + 1) * STRIP]] * subs) for h in range(2)]
    for c in range(clusters):
        copies[c * subs * STRIP:(c + 1) * subs * STRIP] = strips[c % 2]
    copy = pltpu.make_async_copy(copies, packed, ready)
    copy.start()
    parts = [image[:, d * pair:(d + 1) * pair] for d in range(4)]
    for out, values in zip((to_a, to_b, to_c, to_d), by_swap(parts)):
        out[...] = values
    copy.wait()


def pack_places(modes):
    upper = [(0, 0, 7 * modes, 0), (2, 2 * modes, 7 * modes, 7 * modes)]
    lower = [
        (1, modes, 7 * modes, 0), (3, 3 * modes, 6 * modes, 6 * modes),
        (4, 4 * modes, 6 * modes, 9 * modes), (5, 5 * modes, 6 * modes, 11 * modes),
    ]
    return upper, lower


def basis_kernel(
    pair, clusters, basis, image, sign_live, tables, from_a, from_b, from_c, from_d, stacked, applied_first, wide
):
    span = 3 * STRIP
    rows = 4 * pair
    width = clusters * STRIP
    cluster_at = lax.axis_index("clus")
    arrived = by_direction([from_a[...], from_b[...], from_c[...], from_d[...]])
    wide[...] = jnp.zeros_like(wide)
    near = pl.ds(pl.multiple_of((cluster_at + 1) * STRIP, STRIP), span)
    signs = sign_live[...]
    wide[near, 0:rows] = basis[span:2 * span]
    wide[near, rows:2 * rows] = basis[0:span]
    for k in range(2):
        strips = image[k * span:(k + 1) * span]
        wide[near, (2 + k) * rows:(3 + k) * rows] = strips
        wide[near, (4 + k) * rows:(5 + k) * rows] = signs * strips
    for d in range(4):
        lanes = slice(d * pair, (d + 1) * pair)
        sign = sign_live[:, lanes]
        distant = sign * reorder(arrived[d], tables[d])
        at = pl.ds(pl.multiple_of((cluster_at + (1, 1, 0, 2)[d]) * STRIP, STRIP), span)
        for k in range(2):
            begin = (4 + k) * rows + d * pair
            wide[at, begin:begin + pair] -= distant[k * span:(k + 1) * span]
        applied_first[:, lanes] = sign * image[2 * span:, lanes] - distant[2 * span:]
    high, low = halves(wide[2 * STRIP:2 * STRIP + width])
    stacked[0:width] = high
    stacked[width:2 * width] = low
    stacked[2 * width:3 * width] = high


def unpack(half, strips, modes, clusters):
    width = clusters * STRIP
    lane = lax.broadcasted_iota(jnp.int32, (STRIP, 128), 1)
    upper, coupling, with_first, tails = {}, {}, {}, {}

    def put(store, key, values, begin, column):
        tile, offset = divmod(column, 128)
        shift = (offset - begin) % 128
        moved = pltpu.roll(values, shift, 1) if shift else values
        piece = jnp.where((lane >= offset) & (lane < offset + modes), moved, 0.0)
        key = key + (tile,)
        store[key] = store[key] + piece if key in store else piece

    def group(c, h):
        other = c - 1 + h % 3
        return other, (h // 3) * width + other * STRIP

    for c in range(clusters):
        values = strips[c]
        for g, begin, end, at in pack_places(modes)[half]:
            row_cluster, row_at = group(c, g)
            if not 0 <= row_cluster < clusters:
                continue
            for h in range(begin // modes, end // modes):
                source = at + h * modes - begin
                if h == 6:
                    put(coupling, (row_at // STRIP,), values, source, c * STRIP)
                    continue
                other, column = group(c, h)
                if 0 <= other < clusters:
                    put(upper, (row_at // STRIP,), values, source, column)
        for h in range(6):
            other, column = group(c, h)
            if 0 <= other < clusters:
                put(with_first, (half,), values, 12 * modes + h * modes, column)
        put(tails, (half,), values, 19 * modes, c * STRIP)
        put(tails, (2 + half,), values, 18 * modes, c * STRIP)
    return upper, coupling, with_first, tails


def spread(half, strips, modes, clusters, bases, outs):
    stores = unpack(half, [strips[c * STRIP:(c + 1) * STRIP] for c in range(clusters)], modes, clusters)
    for store, base, out in zip(stores, bases, outs):
        for i in range(out.shape[0] // STRIP):
            for t in range(out.shape[1] // 128):
                at = (slice(i * STRIP, (i + 1) * STRIP), slice(t * 128, (t + 1) * 128))
                values = jnp.zeros((STRIP, 128), F32) if base is None else base[at]
                out[at] = values + store[i, t] if (i, t) in store else values


def own_half_kernel(modes, clusters, mine, *outs):
    even_c, _ = parities()
    for half in range(2):
        @pl.when(even_c if half == 0 else jnp.logical_not(even_c))
        def _():
            spread(half, mine, modes, clusters, [None] * 4, outs)


def solve_kernel(
    pair, modes, clusters, other, part_upper, part_couple, part_rows, part_tails, inverse, stacked, rhs, first_part,
    applied_first, weight, sign_live, schur, scalars, to_a, to_b, to_c, to_d, first, applied, second, second_image,
    upper_ref, couple_ref, row_ref, tail_ref, copies, ready
):
    width = clusters * STRIP
    rows = 4 * pair
    even_c, _ = parities()
    for half in range(2):
        @pl.when(even_c if half == 1 else jnp.logical_not(even_c))
        def _():
            spread(
                half, other, modes, clusters, (part_upper, part_couple, part_rows, part_tails),
                (upper_ref, couple_ref, row_ref, tail_ref),
            )

    solver = inverse[...]
    couple_solver = full_product(couple_ref[:, :width], solver)

    def coeffs(straight, weighted):
        both = full_product(jnp.concatenate([straight, weighted]), solver)
        a = both[:PACK]
        return a, both[PACK:] - full_product(a, couple_solver)

    def combine(a, b, tables):
        high, low = halves(jnp.concatenate([a, b]))
        moved = product(jnp.concatenate([high, high, low], axis=1), tables)
        return [[moved[i * PACK:(i + 1) * PACK, k * rows:(k + 1) * rows] for k in range(4)] for i in range(2)]

    tail = tail_ref[:, :width]
    a_first, b_first = coeffs(tail[:PACK], tail[PACK:])
    c_first = jnp.concatenate([a_first, b_first], axis=1)
    upper_matrix = upper_ref[:, :2 * width]
    parts = row_ref[:, :2 * width] - full_product(c_first, upper_matrix) - full_product_t(c_first, upper_matrix)
    a_second, b_second = coeffs(parts[:, width:], parts[:, :width])

    a_of, b_of = combine(a_first, b_first, jnp.concatenate([stacked[:, :2 * rows], stacked[:, 4 * rows:]], axis=1))
    projected = rhs[...] - a_of[0]
    direction = first_part[...] - a_of[1] - b_of[0]
    image = applied_first[...] - a_of[2] - b_of[3]
    heavy = weight[...] * image
    heavy_image = times_matrix(sign_live[...] * heavy, schur[...])

    a_of, b_of = combine(a_second, b_second, stacked[:, :4 * rows])
    image_projected = image - a_of[0]
    last = heavy - a_of[1] - b_of[0]
    last_image = heavy_image - a_of[2] - b_of[3]

    def folded(values):
        return sum(values[:, d * pair:(d + 1) * pair] for d in range(4))

    terms = jnp.concatenate([
        folded(0.5 * (projected * direction)),
        folded(0.5 * (direction * image)),
        folded(0.5 * (projected * last + image_projected * direction)),
        folded(0.5 * (image_projected * last)),
        folded(0.5 * (image * last)),
        folded((sign_live[...] * last) * last_image),
        jnp.zeros((128 - 6 * PACK, pair), F32),
    ])
    ones = jnp.ones((STRIP, 2 * pair), BF16)
    row = lax.dot_general(
        ones, jnp.concatenate(halves(terms), axis=1), (((1,), (1,)), ((), ())), preferred_element_type=F32
    )[0:1]
    copies[...] = jnp.broadcast_to(row[:, None, :], copies.shape)
    copy = pltpu.make_async_copy(copies, scalars, ready)
    copy.start()
    first[...] = direction
    applied[...] = image
    second[...] = last
    second_image[...] = last_image
    parts = [last_image[:, d * pair:(d + 1) * pair] for d in range(4)]
    for out, values in zip((to_a, to_b, to_c, to_d), by_swap(parts)):
        out[...] = values
    copy.wait()


def far_kernel(pair, image, sign_live, tables, from_a, from_b, from_c, from_d, applied):
    arrived = by_direction([from_a[...], from_b[...], from_c[...], from_d[...]])
    for d in range(4):
        lanes = slice(d * pair, (d + 1) * pair)
        applied[:, lanes] = sign_live[:, lanes] * (image[:, lanes] - reorder(arrived[d], tables[d]))


def end_kernel(
    pair, scalars, rhs, first, applied, second, second_applied, multipliers, residual, first_buffer, second_buffer, done
):
    total = jnp.sum(scalars[...], axis=0)
    rho_one, delta_one, cross, square, mixed, delta_last = [
        total if i == 0 else pltpu.roll(total, 128 - i * PACK, 1) for i in range(6)
    ]
    alpha_one = rho_one / delta_one
    rho_two = rho_one - alpha_one * cross + alpha_one * alpha_one * square
    grow = 1.0 + rho_two / rho_one
    delta_two = grow * grow * delta_one - 2.0 * grow * alpha_one * mixed + alpha_one * alpha_one * delta_last
    alpha_two = rho_two / delta_two
    eye = lax.broadcasted_iota(jnp.int32, (PACK, 128), 0) == lax.broadcasted_iota(jnp.int32, (PACK, 128), 1)

    def column(values):
        return jnp.sum(jnp.where(eye, values, 0.0), axis=1, keepdims=True)

    keep = column(alpha_one + alpha_two * grow)
    drop = column(alpha_two * alpha_one)
    results = [
        keep * first[...] - drop * second[...],
        rhs[...] - keep * applied[...] + drop * second_applied[...],
    ]
    copies = []
    for i, (result, out, buffer) in enumerate(zip(results, (multipliers, residual), (first_buffer, second_buffer))):
        for d in range(4):
            buffer[d] = result[:, d * pair:(d + 1) * pair]
        copies.append(pltpu.make_async_copy(buffer, out, done.at[i]))
        copies[-1].start()
    for copy in copies:
        copy.wait()


def call(
    kernel, outs, scratch, *args, place=pltpu.VMEM, first_place=pltpu.VMEM, later_place=pltpu.VMEM, limit=32 * MIB
):
    places = [first_place] + [later_place] * (len(outs) - 1)
    return pl.pallas_call(
        kernel,
        out_shape=[place_out(shape, dtype) for place_out, (shape, dtype) in zip(places, outs)],
        in_specs=[pl.BlockSpec(memory_space=place)] * len(args),
        out_specs=[pl.BlockSpec(memory_space=place_out) for place_out in places],
        scratch_shapes=scratch,
        compiler_params=pltpu.CompilerParams(vmem_limit_bytes=limit),
    )(*[pltpu.with_memory_space_constraint(arg, place) if place is pltpu.HBM else arg for arg in args])


def shards(schur, load, rigid, lengths, partner, coarse_inverse):
    own_load, matrix = load[0, 0], schur[0, 0]
    own_rigid = jnp.swapaxes(rigid[0, 0], 0, 1)
    cases, pair = own_load.shape[1:]
    modes = own_rigid.shape[0]
    clusters, subs = lax.axis_size("clus"), lax.axis_size("sub")
    devices = clusters * subs
    rows = 4 * pair
    width = clusters * STRIP
    span = 3 * STRIP

    wide_inverse = jnp.pad(
        coarse_inverse.reshape(clusters, modes, clusters, modes),
        ((0, 0), (0, STRIP - modes), (0, 0), (0, STRIP - modes)),
    ).reshape(width, width)

    flat = ((cases, rows), F32)
    sent = call(
        functools.partial(start_kernel, pair, modes),
        [((cases + STRIP, pair), F32)] * 4,
        [pltpu.VMEM(own_load.shape, F32), pltpu.VMEM(own_rigid.shape, F32), pltpu.VMEM((4, cases + STRIP, pair), F32),
         pltpu.VMEM((4, pair, pair), BF16), pltpu.SemaphoreType.DMA((6,))],
        own_load, own_rigid, matrix, place=pltpu.HBM,
    )
    arrived = swap(sent)
    matrix, tables, sign_live = call(
        functools.partial(fetch_kernel, pair),
        [((rows, rows), BF16), ((4, pair, pair), BF16), ((1, rows), F32)],
        [pltpu.VMEM((4, pair), jnp.int32), pltpu.VMEM((1, 4), jnp.int32), pltpu.SemaphoreType.DMA((3,))],
        matrix, partner[0, 0], lengths[0], place=pltpu.HBM,
    )

    packed, *images, rhs, first_part, weight, basis, image = call(
        functools.partial(gram_kernel, pair, modes, clusters, subs, cases),
        [((devices * STRIP, 128), F32)] + [((2 * span + cases, pair), F32)] * 4
        + [flat, flat, ((1, rows), F32), ((2 * span, rows), F32), ((2 * span + cases, rows), F32)],
        [pltpu.VMEM((2 * span + 2 * cases, rows), F32), pltpu.VMEM((128, rows), F32),
         pltpu.VMEM((devices * STRIP, 128), F32), pltpu.SemaphoreType.DMA],
        matrix, sign_live, tables, *sent, *arrived, first_place=pltpu.HBM,
    )
    gathered = lax.all_to_all(packed, AXES, 0, 0, tiled=True)
    arrived = swap(images)
    stacked, applied_first = call(
        functools.partial(basis_kernel, pair, clusters),
        [((3 * width, 6 * rows), BF16), flat],
        [pltpu.VMEM((width + 4 * STRIP, 6 * rows), F32)],
        basis, image, sign_live, tables, *arrived,
    )
    gathered, stacked = lax.optimization_barrier((gathered, stacked))

    mine = jnp.sum(gathered.reshape(clusters, subs, STRIP, 128), axis=1).reshape(width, 128)
    other = lax.ppermute(mine, AXES, swap_tables(clusters, subs)[3])
    lanes = max(width, 128)
    shapes = [((2 * width, max(2 * width, 128)), F32), ((width, lanes), F32), ((PACK, max(2 * width, 128)), F32),
              ((2 * PACK, lanes), F32)]
    parts = call(functools.partial(own_half_kernel, modes, clusters), shapes, [], mine)
    scalars, *images, first, applied, second, second_image = call(
        functools.partial(solve_kernel, pair, modes, clusters),
        [((devices, 1, 128), F32)] + [((cases, pair), F32)] * 4 + [flat] * 4,
        [pltpu.VMEM(*shape) for shape in shapes]
        + [pltpu.VMEM((devices, 1, 128), F32), pltpu.SemaphoreType.DMA],
        other, *parts, wide_inverse, stacked, rhs, first_part, applied_first, weight, sign_live, matrix,
        first_place=pltpu.HBM,
    )
    gathered = lax.all_to_all(scalars, AXES, 0, 0, tiled=True)
    arrived = swap(images)
    (second_applied,) = call(
        functools.partial(far_kernel, pair), [flat], [], second_image, sign_live, tables, *arrived
    )
    multipliers, residual = call(
        functools.partial(end_kernel, pair), [((4, cases, pair), F32)] * 2,
        [pltpu.VMEM((4, cases, pair), F32)] * 2 + [pltpu.SemaphoreType.DMA((2,))],
        gathered, rhs, first, applied, second, second_applied, first_place=pltpu.HBM, later_place=pltpu.HBM,
    )
    return (multipliers[None, None], residual[None, None])


def solution(mesh):
    in_specs = (
        P("clus", "sub", None, None),
        P("clus", "sub", None, None, None),
        P("clus", "sub", None, None, None),
        P("clus", "sub", None),
        P("clus", "sub", None, None),
        P(),
    )
    out_specs = (P("clus", "sub", None, None, None), P("clus", "sub", None, None, None))
    return jax.shard_map(shards, mesh=mesh, in_specs=in_specs, out_specs=out_specs, check_vma=False)
```

```python
import functools

import jax
import jax.numpy as jnp
from jax import lax
from jax.experimental import pallas as pl
from jax.experimental.pallas import tpu as pltpu
from jax.sharding import PartitionSpec as P

AXES = ("clus", "sub")
F32 = jnp.float32
BF16 = jnp.bfloat16
FULL = lax.Precision.HIGHEST
STRIP = 8
PACK = 16
MIB = 1024 * 1024


def pair_even(index, count):
    other = index ^ 1
    return other if other < count else index


def pair_odd(index, count):
    other = ((index - 1) ^ 1) + 1
    return other if index > 0 and other < count else index


def swap_tables(clusters, subs):
    sub_even, sub_odd, clus_odd, clus_even = [], [], [], []
    for c in range(clusters):
        for s in range(subs):
            here = c * subs + s
            sub_even.append((here, c * subs + pair_even(s, subs)))
            odd = pair_odd(s, subs)
            target = c * subs + odd if odd != s else pair_even(c, clusters) * subs + s
            sub_odd.append((here, target))
            odd = pair_odd(c, clusters)
            target = odd * subs + s if odd != c else c * subs + pair_even(s, subs)
            clus_odd.append((here, target))
            clus_even.append((here, pair_even(c, clusters) * subs + s))
    return sub_even, sub_odd, clus_odd, clus_even


def swap(buffers):
    tables = swap_tables(lax.axis_size("clus"), lax.axis_size("sub"))
    return [lax.ppermute(buffer, AXES, table) for buffer, table in zip(buffers, tables)]


def parities():
    even_c = lax.rem(lax.axis_index("clus"), 2) == 0
    even_s = lax.rem(lax.axis_index("sub"), 2) == 0
    return even_c, even_s


def by_swap(values):
    even_c, even_s = parities()
    return [
        jnp.where(even_s, values[1], values[0]),
        jnp.where(even_s, values[0], values[1]),
        jnp.where(even_c, values[2], values[3]),
        jnp.where(even_c, values[3], values[2]),
    ]


def by_direction(values):
    even_c, even_s = parities()
    return [
        jnp.where(even_s, values[1], values[0]),
        jnp.where(even_s, values[0], values[1]),
        jnp.where(even_c, values[2], values[3]),
        jnp.where(even_c, values[3], values[2]),
    ]


def halves(values):
    high = values.astype(BF16)
    return high, (values - high.astype(F32)).astype(BF16)


def product(left, right):
    return jnp.dot(left, right, preferred_element_type=F32)


def full_product(left, right):
    return jnp.dot(left, right, preferred_element_type=F32, precision=FULL)


def full_product_t(left, right):
    return lax.dot_general(left, right, (((1,), (1,)), ((), ())), preferred_element_type=F32, precision=FULL)


def reorder(values, table):
    count = values.shape[0]
    high, rest = halves(values)
    low = (values - high.astype(F32) - rest.astype(F32)).astype(BF16)
    moved = product(jnp.concatenate([high, rest, low]), table)
    return moved[:count] + moved[count:2 * count] + moved[2 * count:]


def times_matrix(values, matrix):
    count = values.shape[0]
    both = product(jnp.concatenate(halves(values)), matrix)
    return both[:count] + both[count:]


def products_by_row(left, right):
    count, width = left.shape[0], right.shape[0]
    both = lax.dot_general(
        jnp.concatenate(halves(left)), jnp.concatenate(halves(right)), (((1,), (1,)), ((), ())),
        preferred_element_type=F32,
    )
    wide = jnp.concatenate([both, jnp.zeros((2 * count, 128 - 2 * width), F32)], axis=1)
    return wide[:count] + pltpu.roll(wide[:count], 128 - width, 1) + wide[count:]


def start_kernel(
    pair, modes, load_hbm, rigid_hbm, schur_hbm, to_a, to_b, to_c, to_d, load, rigid, buffer, blocks, arrivals
):
    cases = load.shape[1]
    copies = [
        pltpu.make_async_copy(load_hbm, load, arrivals.at[0]),
        pltpu.make_async_copy(rigid_hbm, rigid, arrivals.at[1]),
    ]
    for d in range(4):
        span = slice(d * pair, (d + 1) * pair)
        copies.append(pltpu.make_async_copy(schur_hbm.at[span, span], blocks.at[d], arrivals.at[2 + d]))
    for copy in copies:
        copy.start()
    eye = lax.broadcasted_iota(jnp.int32, (pair, pair), 0) == lax.broadcasted_iota(jnp.int32, (pair, pair), 1)
    buffer[...] = jnp.zeros_like(buffer)
    for copy in copies:
        copy.wait()
    for d in range(4):
        buffer[d, 0:cases] = load[d]
        buffer[d, cases:cases + modes] = rigid[:, d]
        buffer[d, cases + STRIP - 1:cases + STRIP] = jnp.sum(
            jnp.where(eye, blocks[d].astype(F32), 0.0), axis=0, keepdims=True
        )
    for out, values in zip((to_a, to_b, to_c, to_d), by_swap([buffer[d] for d in range(4)])):
        out[...] = values


def fetch_kernel(
    pair, modes, schur_hbm, partner_hbm, lengths_hbm, coarse_hbm, schur, tables, sign_live, wide_coarse, partner, lengths,
    coarse, arrivals
):
    sources = (partner_hbm, lengths_hbm, coarse_hbm, schur_hbm)
    copies = [
        pltpu.make_async_copy(source, target, arrivals.at[i])
        for i, (source, target) in enumerate(zip(sources, (partner, lengths, coarse, schur)))
    ]
    for copy in copies:
        copy.start()
    shape = (wide_coarse.shape[0], coarse.shape[0])
    wide, order = lax.broadcasted_iota(jnp.int32, shape, 0), lax.broadcasted_iota(jnp.int32, shape, 1)
    mode = wide % STRIP
    place = jnp.where((mode < modes) & (wide // STRIP * modes + mode == order), 1.0, 0.0)
    row = lax.broadcasted_iota(jnp.int32, (pair, pair), 0)
    lane = lax.broadcasted_iota(jnp.int32, (1, pair), 1)
    for copy in copies[:3]:
        copy.wait()
    for d in range(4):
        tables[d] = jnp.where(partner[d:d + 1] == row, 1.0, 0.0).astype(BF16)
        sign_live[:, d * pair:(d + 1) * pair] = jnp.where(lane < lengths[:, d:d + 1], (-1.0, 1.0)[d % 2], 0.0)
    wide_coarse[...] = full_product_t(full_product(place, coarse[...]), place)
    copies[3].wait()


def gram_kernel(
    pair, modes, clusters, subs, cases, schur, sign_live, tables, sent_a, sent_b, sent_c, sent_d, from_a, from_b,
    from_c, from_d, packed, to_a, to_b, to_c, to_d, rhs, first, weight, basis, image, operand, right, copies, ready
):
    span = 3 * STRIP
    own = by_direction([sent_a[...], sent_b[...], sent_c[...], sent_d[...]])
    arrived = by_direction([from_a[...], from_b[...], from_c[...], from_d[...]])
    distant = [reorder(arrived[d], tables[d]) for d in range(4)]
    is_mode = lax.broadcasted_iota(jnp.int32, (STRIP, pair), 0) < modes
    none = jnp.zeros((STRIP, pair), F32)
    right[...] = jnp.zeros_like(right)
    for d in range(4):
        lanes = slice(d * pair, (d + 1) * pair)
        sign = sign_live[:, lanes]
        own_tile, far_tile = own[d][cases:], distant[d][cases:]
        both = own_tile[STRIP - 1:] + far_tile[STRIP - 1:]
        is_live = sign != 0.0
        inverse = jnp.where(is_live, 1.0 / jnp.where(is_live, both, 1.0), 0.0)
        weight[:, lanes] = inverse
        own_rhs = sign * (own[d][:cases] - distant[d][:cases])
        own_first = inverse * own_rhs
        rhs[:, lanes] = own_rhs
        first[:, lanes] = own_first
        operand[2 * span:2 * span + cases, lanes] = sign * own_first
        operand[2 * span + cases:2 * span + 2 * cases, lanes] = sign * own_rhs
        near = jnp.where(is_mode, own_tile - far_tile if d < 2 else own_tile, 0.0) * sign
        far = jnp.where(is_mode, -far_tile, 0.0) * sign
        for slot, values in enumerate((far if d == 2 else none, near, far if d == 3 else none)):
            heavy = slice(slot * STRIP, (slot + 1) * STRIP)
            plain = slice(span + slot * STRIP, span + (slot + 1) * STRIP)
            basis[heavy, lanes] = inverse * values
            basis[plain, lanes] = values
            operand[heavy, lanes] = sign * (inverse * values)
            operand[plain, lanes] = sign * values
        right[6 * modes:7 * modes, lanes] = own_tile[:modes]
    image[...] = times_matrix(operand[0:2 * span + cases], schur[...])
    for g in range(6):
        right[g * modes:(g + 1) * modes] = image[g * STRIP:g * STRIP + modes]
    gram = products_by_row(operand[...], right[...])
    lane = lax.broadcasted_iota(jnp.int32, (STRIP, gram.shape[1]), 1)
    strips = []
    for g in range(6):
        strip = gram[g * STRIP:(g + 1) * STRIP]
        own = (lane >= g * modes) & (lane < (g + 1) * modes)
        if g == 1:
            own = own | (lane >= 6 * modes)
        strips.append(jnp.where(own, 0.5 * strip, strip))
    rows = []
    for row in pack_places(modes):
        total = jnp.zeros_like(strips[0])
        for g, begin, end, at in row:
            piece = strips[g] if at == begin else pltpu.roll(strips[g], (at - begin) % lane.shape[1], 1)
            total = jnp.where((lane >= at) & (lane < at + end - begin), piece, total)
        rows.append(total)
    total = jnp.concatenate(rows)
    lane = lax.broadcasted_iota(jnp.int32, total.shape, 1)
    at = 13 * modes
    with_first = gram[2 * span:2 * span + cases]
    with_rhs = gram[2 * span + cases:2 * span + 2 * cases]
    total = jnp.where(lane >= at, pltpu.roll(with_first, at, 1), total)
    total = jnp.where(lane >= at + 7 * modes, pltpu.roll(with_rhs, at + modes, 1), total)

    strips = [jnp.concatenate([total[h * STRIP:(h + 1) * STRIP]] * subs) for h in range(2)]
    for c in range(clusters):
        copies[c * subs * STRIP:(c + 1) * subs * STRIP] = strips[c % 2]
    copy = pltpu.make_async_copy(copies, packed, ready)
    copy.start()
    parts = [image[:, d * pair:(d + 1) * pair] for d in range(4)]
    for out, values in zip((to_a, to_b, to_c, to_d), by_swap(parts)):
        out[...] = values
    copy.wait()


def pack_places(modes):
    upper = [
        (0, 0, 6 * modes, 0), (2, 2 * modes, 7 * modes, 6 * modes), (1, 6 * modes, 7 * modes, 11 * modes),
    ]
    lower = [
        (1, modes, 7 * modes, 0), (3, 3 * modes, 6 * modes, 6 * modes), (4, 4 * modes, 6 * modes, 9 * modes),
        (5, 5 * modes, 6 * modes, 11 * modes), (2, 6 * modes, 7 * modes, 12 * modes),
    ]
    return upper, lower


def basis_kernel(
    pair, clusters, basis, image, sign_live, tables, from_a, from_b, from_c, from_d, stacked, applied_first, wide
):
    span = 3 * STRIP
    rows = 4 * pair
    width = clusters * STRIP
    cluster_at = lax.axis_index("clus")
    arrived = by_direction([from_a[...], from_b[...], from_c[...], from_d[...]])
    wide[...] = jnp.zeros_like(wide)
    near = pl.ds(pl.multiple_of((cluster_at + 1) * STRIP, STRIP), span)
    signs = sign_live[...]
    wide[near, 0:rows] = basis[span:2 * span]
    wide[near, rows:2 * rows] = basis[0:span]
    for k in range(2):
        strips = image[k * span:(k + 1) * span]
        wide[near, (2 + k) * rows:(3 + k) * rows] = strips
        wide[near, (4 + k) * rows:(5 + k) * rows] = signs * strips
    for d in range(4):
        lanes = slice(d * pair, (d + 1) * pair)
        sign = sign_live[:, lanes]
        distant = sign * reorder(arrived[d], tables[d])
        at = pl.ds(pl.multiple_of((cluster_at + (1, 1, 0, 2)[d]) * STRIP, STRIP), span)
        for k in range(2):
            begin = (4 + k) * rows + d * pair
            wide[at, begin:begin + pair] -= distant[k * span:(k + 1) * span]
        applied_first[:, lanes] = sign * image[2 * span:, lanes] - distant[2 * span:]
    high, low = halves(wide[2 * STRIP:2 * STRIP + width])
    stacked[0:width] = high
    stacked[width:2 * width] = low
    stacked[2 * width:3 * width] = high


def unpack(half, strips, modes, clusters):
    width = clusters * STRIP
    lane = lax.broadcasted_iota(jnp.int32, (STRIP, 128), 1)
    upper, with_first, tails, coupling = {}, {}, {}, {}

    def put(store, key, values, begin, column):
        tile, offset = divmod(column, 128)
        shift = (offset - begin) % 128
        moved = pltpu.roll(values, shift, 1) if shift else values
        piece = jnp.where((lane >= offset) & (lane < offset + modes), moved, 0.0)
        key = key + (tile,)
        store[key] = store[key] + piece if key in store else piece

    def group(c, h):
        other = c - 1 + h % 3
        return other, (h // 3) * width + other * STRIP

    for c in range(clusters):
        values = strips[c]
        for g, begin, end, at in pack_places(modes)[half]:
            row_cluster, row_at = group(c, g)
            if not 0 <= row_cluster < clusters:
                continue
            for h in range(begin // modes, end // modes):
                source = at + h * modes - begin
                if h == 6:
                    put(coupling, (row_at // STRIP,), values, source, c * STRIP)
                    continue
                other, column = group(c, h)
                if 0 <= other < clusters:
                    put(upper, (row_at // STRIP,), values, source, column)
        for h in range(6):
            other, column = group(c, h)
            if 0 <= other < clusters:
                put(with_first, (half,), values, 13 * modes + h * modes, column)
        put(tails, (half,), values, 19 * modes, c * STRIP)
        put(tails, (half,), values, 20 * modes, width + c * STRIP)
    return upper, with_first, tails, coupling


def spread(half, strips, modes, clusters, bases, outs):
    stores = unpack(half, [strips[c * STRIP:(c + 1) * STRIP] for c in range(clusters)], modes, clusters)
    for store, base, out in zip(stores, bases, outs):
        for i in range(out.shape[0] // STRIP):
            for t in range(out.shape[1] // 128):
                at = (slice(i * STRIP, (i + 1) * STRIP), slice(t * 128, (t + 1) * 128))
                values = jnp.zeros((STRIP, 128), F32) if base is None else base[at]
                out[at] = values + store[i, t] if (i, t) in store else values


def stack_rows(values):
    high, low = halves(values)
    return jnp.concatenate([high, low, high])


def stack_lanes(values, second):
    high, low = halves(values)
    return jnp.concatenate([high, low, high] if second else [high, high, low], axis=1)


def own_half_kernel(modes, clusters, mine, inverse, upper, with_first, tails, solver, coupling):
    even_c, _ = parities()
    for half in range(2):
        @pl.when(even_c if half == 0 else jnp.logical_not(even_c))
        def _():
            spread(half, mine, modes, clusters, [None] * 4, (upper, with_first, tails, coupling))
    width = clusters * STRIP
    coarse, half_couple = inverse[...], coupling[:, :width]
    solved = full_product(coarse, half_couple) + full_product_t(coarse, half_couple)
    solved = full_product(solved, coarse)
    solver[...] = stack_rows(jnp.concatenate([
        jnp.concatenate([jnp.zeros_like(coarse), coarse], axis=1),
        jnp.concatenate([coarse, -solved], axis=1),
    ]))


def solve_kernel(
    pair, modes, clusters, other, part_upper, part_first, part_tails, solver, stacked, rhs, first_part,
    applied_first, weight, sign_live, schur, scalars, to_a, to_b, to_c, to_d, first, applied, second, second_image,
    upper_ref, first_ref, tail_ref, copies, ready
):
    width = clusters * STRIP
    rows = 4 * pair
    even_c, _ = parities()
    for half in range(2):
        @pl.when(even_c if half == 1 else jnp.logical_not(even_c))
        def _():
            spread(
                half, other, modes, clusters, (part_upper, part_first, part_tails), (upper_ref, first_ref, tail_ref)
            )

    def combine(coefficients, tables):
        both = jnp.concatenate([coefficients[:, :width], coefficients[:, width:]])
        both = stack_lanes(both, False)
        moved = [product(both, stacked[:, k * rows:(k + 1) * rows]) for k in tables]
        return [part[:PACK] for part in moved], [part[PACK:] for part in moved]

    solve = solver[...]
    upper_matrix = upper_ref[...]
    coefficients = product(stack_lanes(tail_ref[...], False), solve)
    split = stack_lanes(coefficients, False)
    parts = first_ref[...] - product(split, stack_rows(upper_matrix)) - lax.dot_general(
        split, stack_lanes(upper_matrix, True), (((1,), (1,)), ((), ())), preferred_element_type=F32
    )
    later_coefficients = product(stack_lanes(parts, False), solve)

    a_of, b_of = combine(coefficients, (0, 1, 4, 5))
    projected = rhs[...] - a_of[0]
    direction = first_part[...] - a_of[1] - b_of[0]
    image = applied_first[...] - a_of[2] - b_of[3]
    heavy = weight[...] * image
    heavy_image = times_matrix(sign_live[...] * heavy, schur[...])

    a_of, b_of = combine(later_coefficients, (0, 1, 2, 3))
    image_projected = image - a_of[0]
    last = heavy - a_of[1] - b_of[0]
    last_image = heavy_image - a_of[2] - b_of[3]

    def folded(values):
        return sum(values[:, d * pair:(d + 1) * pair] for d in range(4))

    terms = jnp.concatenate([
        folded(0.5 * (projected * direction)),
        folded(0.5 * (direction * image)),
        folded(0.5 * (projected * last + image_projected * direction)),
        folded(0.5 * (image_projected * last)),
        folded(0.5 * (image * last)),
        folded((sign_live[...] * last) * last_image),
    ])
    eye = lax.broadcasted_iota(jnp.int32, terms.shape, 0) == lax.broadcasted_iota(jnp.int32, terms.shape, 1)
    row = jnp.sum(jnp.where(eye, jnp.sum(terms, axis=1, keepdims=True), 0.0), axis=0, keepdims=True)
    copies[...] = jnp.broadcast_to(row[:, None, :], copies.shape)
    copy = pltpu.make_async_copy(copies, scalars, ready)
    copy.start()
    first[...] = direction
    applied[...] = image
    second[...] = last
    second_image[...] = last_image
    parts = [last_image[:, d * pair:(d + 1) * pair] for d in range(4)]
    for out, values in zip((to_a, to_b, to_c, to_d), by_swap(parts)):
        out[...] = values
    copy.wait()


def far_kernel(pair, image, sign_live, tables, from_a, from_b, from_c, from_d, applied):
    arrived = by_direction([from_a[...], from_b[...], from_c[...], from_d[...]])
    for d in range(4):
        lanes = slice(d * pair, (d + 1) * pair)
        applied[:, lanes] = sign_live[:, lanes] * (image[:, lanes] - reorder(arrived[d], tables[d]))


def end_kernel(
    pair, scalars, rhs, first, applied, second, second_applied, multipliers, residual, first_buffer, second_buffer, done
):
    total = jnp.sum(scalars[...], axis=0)
    rho_one, delta_one, cross, square, mixed, delta_last = [
        total if i == 0 else pltpu.roll(total, 128 - i * PACK, 1) for i in range(6)
    ]
    alpha_one = rho_one / delta_one
    rho_two = rho_one - alpha_one * cross + alpha_one * alpha_one * square
    grow = 1.0 + rho_two / rho_one
    delta_two = grow * grow * delta_one - 2.0 * grow * alpha_one * mixed + alpha_one * alpha_one * delta_last
    alpha_two = rho_two / delta_two
    eye = lax.broadcasted_iota(jnp.int32, (PACK, 128), 0) == lax.broadcasted_iota(jnp.int32, (PACK, 128), 1)

    def column(values):
        return jnp.sum(jnp.where(eye, values, 0.0), axis=1, keepdims=True)

    keep = column(alpha_one + alpha_two * grow)
    drop = column(alpha_two * alpha_one)
    results = [
        keep * first[...] - drop * second[...],
        rhs[...] - keep * applied[...] + drop * second_applied[...],
    ]
    copies = []
    for i, (result, out, buffer) in enumerate(zip(results, (multipliers, residual), (first_buffer, second_buffer))):
        for d in range(4):
            buffer[d] = result[:, d * pair:(d + 1) * pair]
        copies.append(pltpu.make_async_copy(buffer, out, done.at[i]))
        copies[-1].start()
    for copy in copies:
        copy.wait()


def call(
    kernel, outs, scratch, *args, place=pltpu.VMEM, first_place=pltpu.VMEM, later_place=pltpu.VMEM, limit=32 * MIB
):
    places = [first_place] + [later_place] * (len(outs) - 1)
    return pl.pallas_call(
        kernel,
        out_shape=[place_out(shape, dtype) for place_out, (shape, dtype) in zip(places, outs)],
        in_specs=[pl.BlockSpec(memory_space=place)] * len(args),
        out_specs=[pl.BlockSpec(memory_space=place_out) for place_out in places],
        scratch_shapes=scratch,
        compiler_params=pltpu.CompilerParams(vmem_limit_bytes=limit),
    )(*[pltpu.with_memory_space_constraint(arg, place) if place is pltpu.HBM else arg for arg in args])


def shards(schur, load, rigid, lengths, partner, coarse_inverse):
    own_load, matrix = load[0, 0], schur[0, 0]
    own_rigid = jnp.swapaxes(rigid[0, 0], 0, 1)
    cases, pair = own_load.shape[1:]
    modes = own_rigid.shape[0]
    clusters, subs = lax.axis_size("clus"), lax.axis_size("sub")
    devices = clusters * subs
    rows = 4 * pair
    width = clusters * STRIP
    span = 3 * STRIP

    flat = ((cases, rows), F32)
    sent = call(
        functools.partial(start_kernel, pair, modes),
        [((cases + STRIP, pair), F32)] * 4,
        [pltpu.VMEM(own_load.shape, F32), pltpu.VMEM(own_rigid.shape, F32), pltpu.VMEM((4, cases + STRIP, pair), F32),
         pltpu.VMEM((4, pair, pair), BF16), pltpu.SemaphoreType.DMA((6,))],
        own_load, own_rigid, matrix, place=pltpu.HBM,
    )
    arrived = swap(sent)
    matrix, tables, sign_live, wide_inverse = call(
        functools.partial(fetch_kernel, pair, modes),
        [((rows, rows), BF16), ((4, pair, pair), BF16), ((1, rows), F32), ((width, width), F32)],
        [pltpu.VMEM((4, pair), jnp.int32), pltpu.VMEM((1, 4), jnp.int32), pltpu.VMEM(coarse_inverse.shape, F32),
         pltpu.SemaphoreType.DMA((4,))],
        matrix, partner[0, 0], lengths[0], coarse_inverse, place=pltpu.HBM,
    )

    packed, *images, rhs, first_part, weight, basis, image = call(
        functools.partial(gram_kernel, pair, modes, clusters, subs, cases),
        [((devices * STRIP, 128), F32)] + [((2 * span + cases, pair), F32)] * 4
        + [flat, flat, ((1, rows), F32), ((2 * span, rows), F32), ((2 * span + cases, rows), F32)],
        [pltpu.VMEM((2 * span + 2 * cases, rows), F32), pltpu.VMEM((48, rows), F32),
         pltpu.VMEM((devices * STRIP, 128), F32), pltpu.SemaphoreType.DMA],
        matrix, sign_live, tables, *sent, *arrived, first_place=pltpu.HBM,
    )
    gathered = lax.all_to_all(packed, AXES, 0, 0, tiled=True)
    arrived = swap(images)
    stacked, applied_first = call(
        functools.partial(basis_kernel, pair, clusters),
        [((3 * width, 6 * rows), BF16), flat],
        [pltpu.VMEM((width + 4 * STRIP, 6 * rows), F32)],
        basis, image, sign_live, tables, *arrived,
    )
    gathered, stacked = lax.optimization_barrier((gathered, stacked))

    mine = jnp.sum(gathered.reshape(clusters, subs, STRIP, 128), axis=1).reshape(width, 128)
    other = lax.ppermute(mine, AXES, swap_tables(clusters, subs)[3])
    shapes = [((2 * width, 2 * width), F32), ((PACK, 2 * width), F32), ((PACK, 2 * width), F32)]
    parts = call(
        functools.partial(own_half_kernel, modes, clusters), shapes + [((6 * width, 2 * width), BF16)],
        [pltpu.VMEM((width, max(width, 128)), F32)], mine, wide_inverse,
    )
    scalars, *images, first, applied, second, second_image = call(
        functools.partial(solve_kernel, pair, modes, clusters),
        [((devices, 1, 128), F32)] + [((cases, pair), F32)] * 4 + [flat] * 4,
        [pltpu.VMEM(*shape) for shape in shapes]
        + [pltpu.VMEM((devices, 1, 128), F32), pltpu.SemaphoreType.DMA],
        other, *parts, stacked, rhs, first_part, applied_first, weight, sign_live, matrix,
        first_place=pltpu.HBM,
    )
    gathered = lax.all_to_all(scalars, AXES, 0, 0, tiled=True)
    arrived = swap(images)
    (second_applied,) = call(
        functools.partial(far_kernel, pair), [flat], [], second_image, sign_live, tables, *arrived
    )
    multipliers, residual = call(
        functools.partial(end_kernel, pair), [((4, cases, pair), F32)] * 2,
        [pltpu.VMEM((4, cases, pair), F32)] * 2 + [pltpu.SemaphoreType.DMA((2,))],
        gathered, rhs, first, applied, second, second_applied, first_place=pltpu.HBM, later_place=pltpu.HBM,
    )
    return (multipliers[None, None], residual[None, None])


def solution(mesh):
    in_specs = (
        P("clus", "sub", None, None),
        P("clus", "sub", None, None, None),
        P("clus", "sub", None, None, None),
        P("clus", "sub", None),
        P("clus", "sub", None, None),
        P(),
    )
    out_specs = (P("clus", "sub", None, None, None), P("clus", "sub", None, None, None))
    return jax.shard_map(shards, mesh=mesh, in_specs=in_specs, out_specs=out_specs, check_vma=False)
```

```python
import functools

import jax
import jax.numpy as jnp
from jax import lax
from jax.experimental import pallas as pl
from jax.experimental.pallas import tpu as pltpu
from jax.sharding import PartitionSpec as P

AXES = ("clus", "sub")
SWAPS = ("sub_odd", "sub_even", "clus_odd", "clus_even")
F32 = jnp.float32
BF16 = jnp.bfloat16
FULL = lax.Precision.HIGHEST
STRIP = 8
PACK = 16
MIB = 1024 * 1024


def pair_even(index, count):
    other = index ^ 1
    return other if other < count else index


def pair_odd(index, count):
    other = ((index - 1) ^ 1) + 1
    return other if index > 0 and other < count else index


def swap_tables(clusters, subs):
    tables = {"sub_even": [], "sub_odd": [], "clus_even": [], "clus_odd": []}
    for c in range(clusters):
        for s in range(subs):
            odd_c, odd_s = pair_odd(c, clusters), pair_odd(s, subs)
            even_c, even_s = pair_even(c, clusters), pair_even(s, subs)
            targets = {
                "sub_even": (c, even_s),
                "sub_odd": (c, odd_s) if odd_s != s else (even_c, s),
                "clus_even": (even_c, s),
                "clus_odd": (odd_c, s) if odd_c != c else (c, even_s),
            }
            for name, (to_c, to_s) in targets.items():
                tables[name].append((c * subs + s, to_c * subs + to_s))
    return tables


def swap(buffers):
    tables = swap_tables(lax.axis_size("clus"), lax.axis_size("sub"))
    return [lax.ppermute(buffer, AXES, tables[name]) for buffer, name in zip(buffers, SWAPS)]


def parities():
    even_c = lax.rem(lax.axis_index("clus"), 2) == 0
    even_s = lax.rem(lax.axis_index("sub"), 2) == 0
    return even_c, even_s


def by_swap(values):
    even_c, even_s = parities()
    named = {
        "sub_even": jnp.where(even_s, values[1], values[0]),
        "sub_odd": jnp.where(even_s, values[0], values[1]),
        "clus_even": jnp.where(even_c, values[3], values[2]),
        "clus_odd": jnp.where(even_c, values[2], values[3]),
    }
    return [named[name] for name in SWAPS]


def by_direction(values):
    even_c, even_s = parities()
    named = dict(zip(SWAPS, values))
    return [
        jnp.where(even_s, named["sub_odd"], named["sub_even"]),
        jnp.where(even_s, named["sub_even"], named["sub_odd"]),
        jnp.where(even_c, named["clus_odd"], named["clus_even"]),
        jnp.where(even_c, named["clus_even"], named["clus_odd"]),
    ]


def halves(values):
    high = values.astype(BF16)
    return high, (values - high.astype(F32)).astype(BF16)


def product(left, right):
    return jnp.dot(left, right, preferred_element_type=F32)


def full_product(left, right):
    return jnp.dot(left, right, preferred_element_type=F32, precision=FULL)


def full_product_t(left, right):
    return lax.dot_general(left, right, (((1,), (1,)), ((), ())), preferred_element_type=F32, precision=FULL)


def reorder(values, table):
    count = values.shape[0]
    high, rest = halves(values)
    low = (values - high.astype(F32) - rest.astype(F32)).astype(BF16)
    moved = product(jnp.concatenate([high, rest, low]), table)
    return moved[:count] + moved[count:2 * count] + moved[2 * count:]


def times_matrix(values, matrix):
    count = values.shape[0]
    both = product(jnp.concatenate(halves(values)), matrix)
    return both[:count] + both[count:]


def products_by_row(left, right):
    count, width = left.shape[0], right.shape[0]
    both = lax.dot_general(
        jnp.concatenate(halves(left)), jnp.concatenate(halves(right)), (((1,), (1,)), ((), ())),
        preferred_element_type=F32,
    )
    wide = jnp.concatenate([both, jnp.zeros((2 * count, 128 - 2 * width), F32)], axis=1)
    return wide[:count] + pltpu.roll(wide[:count], 128 - width, 1) + wide[count:]


def start_kernel(
    pair, modes, load_hbm, rigid_hbm, schur_hbm, to_a, to_b, to_c, to_d, load, rigid, blocks, arrivals
):
    cases = load.shape[1]
    copies = [
        pltpu.make_async_copy(load_hbm, load, arrivals.at[0]),
        pltpu.make_async_copy(rigid_hbm, rigid.at[0:modes], arrivals.at[1]),
    ]
    for d in range(4):
        span = slice(d * pair, (d + 1) * pair)
        copies.append(pltpu.make_async_copy(schur_hbm.at[span, span], blocks.at[d], arrivals.at[2 + d]))
    for copy in copies:
        copy.start()
    eye = lax.broadcasted_iota(jnp.int32, (pair, pair), 0) == lax.broadcasted_iota(jnp.int32, (pair, pair), 1)
    row = lax.broadcasted_iota(jnp.int32, (STRIP, pair), 0)
    for copy in copies:
        copy.wait()
    tiles = []
    for d in range(4):
        diag = jnp.sum(jnp.where(eye, blocks[d].astype(F32), 0.0), axis=0, keepdims=True)
        tiles.append(jnp.where(row == STRIP - 1, diag, jnp.where(row < modes, rigid[:, d], 0.0)))
    loads = by_swap([load[d] for d in range(4)])
    for out, own_load, tile in zip((to_a, to_b, to_c, to_d), loads, by_swap(tiles)):
        out[0:cases] = own_load
        out[cases:cases + STRIP] = tile


def fetch_kernel(
    pair, modes, schur_hbm, partner_hbm, lengths_hbm, coarse_hbm, schur, tables, sign_live, wide_coarse, partner, lengths,
    coarse, arrivals
):
    sources = (partner_hbm, lengths_hbm, coarse_hbm, schur_hbm)
    copies = [
        pltpu.make_async_copy(source, target, arrivals.at[i])
        for i, (source, target) in enumerate(zip(sources, (partner, lengths, coarse, schur)))
    ]
    for copy in copies:
        copy.start()
    shape = (wide_coarse.shape[0], coarse.shape[0])
    wide, order = lax.broadcasted_iota(jnp.int32, shape, 0), lax.broadcasted_iota(jnp.int32, shape, 1)
    mode = wide % STRIP
    place = jnp.where((mode < modes) & (wide // STRIP * modes + mode == order), 1.0, 0.0)
    row = lax.broadcasted_iota(jnp.int32, (pair, pair), 0)
    lane = lax.broadcasted_iota(jnp.int32, (1, pair), 1)
    for copy in copies[:3]:
        copy.wait()
    for d in range(4):
        tables[d] = jnp.where(partner[d:d + 1] == row, 1.0, 0.0).astype(BF16)
        sign_live[:, d * pair:(d + 1) * pair] = jnp.where(lane < lengths[:, d:d + 1], (-1.0, 1.0)[d % 2], 0.0)
    wide_coarse[...] = full_product_t(full_product(place, coarse[...]), place)
    copies[3].wait()


def gram_kernel(
    pair, modes, clusters, subs, cases, schur, sign_live, tables, sent_a, sent_b, sent_c, sent_d, from_a, from_b,
    from_c, from_d, packed, to_a, to_b, to_c, to_d, rhs, first, weight, basis, image, operand, right, copies, ready
):
    span = 3 * STRIP
    own = by_direction([sent_a[...], sent_b[...], sent_c[...], sent_d[...]])
    arrived = by_direction([from_a[...], from_b[...], from_c[...], from_d[...]])
    distant = [reorder(arrived[d], tables[d]) for d in range(4)]
    is_mode = lax.broadcasted_iota(jnp.int32, (STRIP, pair), 0) < modes
    none = jnp.zeros((STRIP, pair), F32)
    right[...] = jnp.zeros_like(right)
    for d in range(4):
        lanes = slice(d * pair, (d + 1) * pair)
        sign = sign_live[:, lanes]
        own_tile, far_tile = own[d][cases:], distant[d][cases:]
        both = own_tile[STRIP - 1:] + far_tile[STRIP - 1:]
        is_live = sign != 0.0
        inverse = jnp.where(is_live, 1.0 / jnp.where(is_live, both, 1.0), 0.0)
        weight[:, lanes] = inverse
        own_rhs = sign * (own[d][:cases] - distant[d][:cases])
        own_first = inverse * own_rhs
        rhs[:, lanes] = own_rhs
        first[:, lanes] = own_first
        operand[2 * span:2 * span + cases, lanes] = sign * own_first
        operand[2 * span + cases:2 * span + 2 * cases, lanes] = sign * own_rhs
        near = jnp.where(is_mode, own_tile - far_tile if d < 2 else own_tile, 0.0) * sign
        far = jnp.where(is_mode, -far_tile, 0.0) * sign
        for slot, values in enumerate((far if d == 2 else none, near, far if d == 3 else none)):
            heavy = slice(slot * STRIP, (slot + 1) * STRIP)
            plain = slice(span + slot * STRIP, span + (slot + 1) * STRIP)
            basis[heavy, lanes] = inverse * values
            basis[plain, lanes] = values
            operand[heavy, lanes] = sign * (inverse * values)
            operand[plain, lanes] = sign * values
        right[6 * modes:7 * modes, lanes] = own_tile[:modes]
    image[...] = times_matrix(operand[0:2 * span + cases], schur[...])
    for g in range(6):
        right[g * modes:(g + 1) * modes] = image[g * STRIP:g * STRIP + modes]
    gram = products_by_row(operand[...], right[...])
    lane = lax.broadcasted_iota(jnp.int32, (STRIP, gram.shape[1]), 1)
    strips = []
    for g in range(6):
        strip = gram[g * STRIP:(g + 1) * STRIP]
        own = (lane >= g * modes) & (lane < (g + 1) * modes)
        if g == 1:
            own = own | (lane >= 6 * modes)
        strips.append(jnp.where(own, 0.5 * strip, strip))
    rows = []
    for row in pack_places(modes):
        total = jnp.zeros_like(strips[0])
        for g, begin, end, at in row:
            piece = strips[g] if at == begin else pltpu.roll(strips[g], (at - begin) % lane.shape[1], 1)
            total = jnp.where((lane >= at) & (lane < at + end - begin), piece, total)
        rows.append(total)
    total = jnp.concatenate(rows)
    lane = lax.broadcasted_iota(jnp.int32, total.shape, 1)
    at = 13 * modes
    with_first = gram[2 * span:2 * span + cases]
    with_rhs = gram[2 * span + cases:2 * span + 2 * cases]
    total = jnp.where(lane >= at, pltpu.roll(with_first, at, 1), total)
    total = jnp.where(lane >= at + 7 * modes, pltpu.roll(with_rhs, at + modes, 1), total)

    strips = [jnp.concatenate([total[h * STRIP:(h + 1) * STRIP]] * subs) for h in range(2)]
    for c in range(clusters):
        copies[c * subs * STRIP:(c + 1) * subs * STRIP] = strips[c % 2]
    copy = pltpu.make_async_copy(copies, packed, ready)
    copy.start()
    parts = [image[:, d * pair:(d + 1) * pair] for d in range(4)]
    for out, values in zip((to_a, to_b, to_c, to_d), by_swap(parts)):
        out[...] = values
    copy.wait()


def pack_places(modes):
    upper = [
        (0, 0, 6 * modes, 0), (2, 2 * modes, 7 * modes, 6 * modes), (1, 6 * modes, 7 * modes, 11 * modes),
    ]
    lower = [
        (1, modes, 7 * modes, 0), (3, 3 * modes, 6 * modes, 6 * modes), (4, 4 * modes, 6 * modes, 9 * modes),
        (5, 5 * modes, 6 * modes, 11 * modes), (2, 6 * modes, 7 * modes, 12 * modes),
    ]
    return upper, lower


def basis_kernel(
    pair, clusters, basis, image, sign_live, tables, from_a, from_b, from_c, from_d, stacked, applied_first, wide
):
    span = 3 * STRIP
    rows = 4 * pair
    width = clusters * STRIP
    cluster_at = lax.axis_index("clus")
    arrived = by_direction([from_a[...], from_b[...], from_c[...], from_d[...]])
    wide[...] = jnp.zeros_like(wide)
    near = pl.ds(pl.multiple_of((cluster_at + 1) * STRIP, STRIP), span)
    signs = sign_live[...]
    wide[near, 0:rows] = basis[span:2 * span]
    wide[near, rows:2 * rows] = basis[0:span]
    for k in range(2):
        strips = image[k * span:(k + 1) * span]
        wide[near, (2 + k) * rows:(3 + k) * rows] = strips
        wide[near, (4 + k) * rows:(5 + k) * rows] = signs * strips
    for d in range(4):
        lanes = slice(d * pair, (d + 1) * pair)
        sign = sign_live[:, lanes]
        distant = sign * reorder(arrived[d], tables[d])
        at = pl.ds(pl.multiple_of((cluster_at + (1, 1, 0, 2)[d]) * STRIP, STRIP), span)
        for k in range(2):
            begin = (4 + k) * rows + d * pair
            wide[at, begin:begin + pair] -= distant[k * span:(k + 1) * span]
        applied_first[:, lanes] = sign * image[2 * span:, lanes] - distant[2 * span:]
    high, low = halves(wide[2 * STRIP:2 * STRIP + width])
    stacked[0:width] = high
    stacked[width:2 * width] = low
    stacked[2 * width:3 * width] = high


def unpack(half, strips, modes, clusters):
    width = clusters * STRIP
    lane = lax.broadcasted_iota(jnp.int32, (STRIP, 128), 1)
    upper, with_first, tails, coupling = {}, {}, {}, {}

    def put(store, key, values, begin, column):
        tile, offset = divmod(column, 128)
        shift = (offset - begin) % 128
        moved = pltpu.roll(values, shift, 1) if shift else values
        piece = jnp.where((lane >= offset) & (lane < offset + modes), moved, 0.0)
        key = key + (tile,)
        store[key] = store[key] + piece if key in store else piece

    def group(c, h):
        other = c - 1 + h % 3
        return other, (h // 3) * width + other * STRIP

    for c in range(clusters):
        values = strips[c]
        for g, begin, end, at in pack_places(modes)[half]:
            row_cluster, row_at = group(c, g)
            if not 0 <= row_cluster < clusters:
                continue
            for h in range(begin // modes, end // modes):
                source = at + h * modes - begin
                if h == 6:
                    put(coupling, (row_at // STRIP,), values, source, c * STRIP)
                    continue
                other, column = group(c, h)
                if 0 <= other < clusters:
                    put(upper, (row_at // STRIP,), values, source, column)
        for h in range(6):
            other, column = group(c, h)
            if 0 <= other < clusters:
                put(with_first, (half,), values, 13 * modes + h * modes, column)
        put(tails, (half,), values, 19 * modes, c * STRIP)
        put(tails, (half,), values, 20 * modes, width + c * STRIP)
    return upper, with_first, tails, coupling


def spread(half, strips, modes, clusters, bases, outs):
    stores = unpack(half, [strips[c * STRIP:(c + 1) * STRIP] for c in range(clusters)], modes, clusters)
    for store, base, out in zip(stores, bases, outs):
        for i in range(out.shape[0] // STRIP):
            for t in range(out.shape[1] // 128):
                at = (slice(i * STRIP, (i + 1) * STRIP), slice(t * 128, (t + 1) * 128))
                values = jnp.zeros((STRIP, 128), F32) if base is None else base[at]
                out[at] = values + store[i, t] if (i, t) in store else values


def stack_rows(values):
    high, low = halves(values)
    return jnp.concatenate([high, low, high])


def stack_lanes(values, second):
    high, low = halves(values)
    return jnp.concatenate([high, low, high] if second else [high, high, low], axis=1)


def own_half_kernel(modes, clusters, mine, inverse, upper, with_first, tails, solver, coupling):
    even_c, _ = parities()
    for half in range(2):
        @pl.when(even_c if half == 0 else jnp.logical_not(even_c))
        def _():
            spread(half, mine, modes, clusters, [None] * 4, (upper, with_first, tails, coupling))
    width = clusters * STRIP
    coarse, half_couple = inverse[...], coupling[:, :width]
    solved = full_product(coarse, half_couple) + full_product_t(coarse, half_couple)
    solved = full_product(solved, coarse)
    solver[...] = stack_rows(jnp.concatenate([
        jnp.concatenate([jnp.zeros_like(coarse), coarse], axis=1),
        jnp.concatenate([coarse, -solved], axis=1),
    ]))


def solve_kernel(
    pair, modes, clusters, other, part_upper, part_first, part_tails, solver, stacked, rhs, first_part,
    applied_first, weight, sign_live, schur, scalars, to_a, to_b, to_c, to_d, first, applied, second, second_image,
    upper_ref, first_ref, tail_ref, copies, ready
):
    width = clusters * STRIP
    rows = 4 * pair
    even_c, _ = parities()
    for half in range(2):
        @pl.when(even_c if half == 1 else jnp.logical_not(even_c))
        def _():
            spread(
                half, other, modes, clusters, (part_upper, part_first, part_tails), (upper_ref, first_ref, tail_ref)
            )

    def combine(coefficients, tables):
        both = jnp.concatenate([coefficients[:, :width], coefficients[:, width:]])
        both = stack_lanes(both, False)
        moved = [product(both, stacked[:, k * rows:(k + 1) * rows]) for k in tables]
        return [part[:PACK] for part in moved], [part[PACK:] for part in moved]

    solve = solver[...]
    upper_matrix = upper_ref[...]
    coefficients = product(stack_lanes(tail_ref[...], False), solve)
    split = stack_lanes(coefficients, False)
    parts = first_ref[...] - product(split, stack_rows(upper_matrix)) - lax.dot_general(
        split, stack_lanes(upper_matrix, True), (((1,), (1,)), ((), ())), preferred_element_type=F32
    )
    later_coefficients = product(stack_lanes(parts, False), solve)

    a_of, b_of = combine(coefficients, (0, 1, 4, 5))
    projected = rhs[...] - a_of[0]
    direction = first_part[...] - a_of[1] - b_of[0]
    image = applied_first[...] - a_of[2] - b_of[3]
    heavy = weight[...] * image
    heavy_image = times_matrix(sign_live[...] * heavy, schur[...])

    a_of, b_of = combine(later_coefficients, (0, 1, 2, 3))
    image_projected = image - a_of[0]
    last = heavy - a_of[1] - b_of[0]
    last_image = heavy_image - a_of[2] - b_of[3]

    def folded(values):
        return sum(values[:, d * pair:(d + 1) * pair] for d in range(4))

    terms = jnp.concatenate([
        folded(0.5 * (projected * direction)),
        folded(0.5 * (direction * image)),
        folded(0.5 * (projected * last + image_projected * direction)),
        folded(0.5 * (image_projected * last)),
        folded(0.5 * (image * last)),
        folded((sign_live[...] * last) * last_image),
    ])
    eye = lax.broadcasted_iota(jnp.int32, terms.shape, 0) == lax.broadcasted_iota(jnp.int32, terms.shape, 1)
    row = jnp.sum(jnp.where(eye, jnp.sum(terms, axis=1, keepdims=True), 0.0), axis=0, keepdims=True)
    copies[...] = jnp.broadcast_to(row[:, None, :], copies.shape)
    copy = pltpu.make_async_copy(copies, scalars, ready)
    copy.start()
    first[...] = direction
    applied[...] = image
    second[...] = last
    second_image[...] = last_image
    parts = [last_image[:, d * pair:(d + 1) * pair] for d in range(4)]
    for out, values in zip((to_a, to_b, to_c, to_d), by_swap(parts)):
        out[...] = values
    copy.wait()


def far_kernel(pair, image, sign_live, tables, from_a, from_b, from_c, from_d, applied):
    arrived = by_direction([from_a[...], from_b[...], from_c[...], from_d[...]])
    for d in range(4):
        lanes = slice(d * pair, (d + 1) * pair)
        applied[:, lanes] = sign_live[:, lanes] * (image[:, lanes] - reorder(arrived[d], tables[d]))


def end_kernel(
    pair, scalars, rhs, first, applied, second, second_applied, multipliers, residual, first_buffer, second_buffer, done
):
    total = jnp.sum(scalars[...], axis=0)
    rho_one, delta_one, cross, square, mixed, delta_last = [
        total if i == 0 else pltpu.roll(total, 128 - i * PACK, 1) for i in range(6)
    ]
    alpha_one = rho_one / delta_one
    rho_two = rho_one - alpha_one * cross + alpha_one * alpha_one * square
    grow = 1.0 + rho_two / rho_one
    delta_two = grow * grow * delta_one - 2.0 * grow * alpha_one * mixed + alpha_one * alpha_one * delta_last
    alpha_two = rho_two / delta_two
    eye = lax.broadcasted_iota(jnp.int32, (PACK, 128), 0) == lax.broadcasted_iota(jnp.int32, (PACK, 128), 1)

    def column(values):
        return jnp.sum(jnp.where(eye, values, 0.0), axis=1, keepdims=True)

    keep = column(alpha_one + alpha_two * grow)
    drop = column(alpha_two * alpha_one)
    results = [
        keep * first[...] - drop * second[...],
        rhs[...] - keep * applied[...] + drop * second_applied[...],
    ]
    copies = []
    for i, (result, out, buffer) in enumerate(zip(results, (multipliers, residual), (first_buffer, second_buffer))):
        for d in range(4):
            buffer[d] = result[:, d * pair:(d + 1) * pair]
        copies.append(pltpu.make_async_copy(buffer, out, done.at[i]))
        copies[-1].start()
    for copy in copies:
        copy.wait()


def call(
    kernel, outs, scratch, *args, place=pltpu.VMEM, first_place=pltpu.VMEM, later_place=pltpu.VMEM, limit=32 * MIB
):
    places = [first_place] + [later_place] * (len(outs) - 1)
    return pl.pallas_call(
        kernel,
        out_shape=[place_out(shape, dtype) for place_out, (shape, dtype) in zip(places, outs)],
        in_specs=[pl.BlockSpec(memory_space=place)] * len(args),
        out_specs=[pl.BlockSpec(memory_space=place_out) for place_out in places],
        scratch_shapes=scratch,
        compiler_params=pltpu.CompilerParams(vmem_limit_bytes=limit),
    )(*[pltpu.with_memory_space_constraint(arg, place) if place is pltpu.HBM else arg for arg in args])


def shards(schur, load, rigid, lengths, partner, coarse_inverse):
    own_load, matrix = load[0, 0], schur[0, 0]
    own_rigid = jnp.swapaxes(rigid[0, 0], 0, 1)
    cases, pair = own_load.shape[1:]
    modes = own_rigid.shape[0]
    clusters, subs = lax.axis_size("clus"), lax.axis_size("sub")
    devices = clusters * subs
    rows = 4 * pair
    width = clusters * STRIP
    span = 3 * STRIP

    flat = ((cases, rows), F32)
    sent = call(
        functools.partial(start_kernel, pair, modes),
        [((cases + STRIP, pair), F32)] * 4,
        [pltpu.VMEM(own_load.shape, F32), pltpu.VMEM((STRIP, 4, pair), F32),
         pltpu.VMEM((4, pair, pair), BF16), pltpu.SemaphoreType.DMA((6,))],
        own_load, own_rigid, matrix, place=pltpu.HBM,
    )
    arrived = swap(sent)
    matrix, tables, sign_live, wide_inverse = call(
        functools.partial(fetch_kernel, pair, modes),
        [((rows, rows), BF16), ((4, pair, pair), BF16), ((1, rows), F32), ((width, width), F32)],
        [pltpu.VMEM((4, pair), jnp.int32), pltpu.VMEM((1, 4), jnp.int32), pltpu.VMEM(coarse_inverse.shape, F32),
         pltpu.SemaphoreType.DMA((4,))],
        matrix, partner[0, 0], lengths[0], coarse_inverse, place=pltpu.HBM,
    )

    packed, *images, rhs, first_part, weight, basis, image = call(
        functools.partial(gram_kernel, pair, modes, clusters, subs, cases),
        [((devices * STRIP, 128), F32)] + [((2 * span + cases, pair), F32)] * 4
        + [flat, flat, ((1, rows), F32), ((2 * span, rows), F32), ((2 * span + cases, rows), F32)],
        [pltpu.VMEM((2 * span + 2 * cases, rows), F32), pltpu.VMEM((48, rows), F32),
         pltpu.VMEM((devices * STRIP, 128), F32), pltpu.SemaphoreType.DMA],
        matrix, sign_live, tables, *sent, *arrived, first_place=pltpu.HBM,
    )
    gathered = lax.all_to_all(packed, AXES, 0, 0, tiled=True)
    arrived = swap(images)
    stacked, applied_first = call(
        functools.partial(basis_kernel, pair, clusters),
        [((3 * width, 6 * rows), BF16), flat],
        [pltpu.VMEM((width + 4 * STRIP, 6 * rows), F32)],
        basis, image, sign_live, tables, *arrived,
    )
    gathered, stacked = lax.optimization_barrier((gathered, stacked))

    mine = jnp.sum(gathered.reshape(clusters, subs, STRIP, 128), axis=1).reshape(width, 128)
    other = lax.ppermute(mine, AXES, swap_tables(clusters, subs)["clus_even"])
    shapes = [((2 * width, 2 * width), F32), ((PACK, 2 * width), F32), ((PACK, 2 * width), F32)]
    parts = call(
        functools.partial(own_half_kernel, modes, clusters), shapes + [((6 * width, 2 * width), BF16)],
        [pltpu.VMEM((width, max(width, 128)), F32)], mine, wide_inverse,
    )
    scalars, *images, first, applied, second, second_image = call(
        functools.partial(solve_kernel, pair, modes, clusters),
        [((devices, 1, 128), F32)] + [((cases, pair), F32)] * 4 + [flat] * 4,
        [pltpu.VMEM(*shape) for shape in shapes]
        + [pltpu.VMEM((devices, 1, 128), F32), pltpu.SemaphoreType.DMA],
        other, *parts, stacked, rhs, first_part, applied_first, weight, sign_live, matrix,
        first_place=pltpu.HBM,
    )
    gathered = lax.all_to_all(scalars, AXES, 0, 0, tiled=True)
    arrived = swap(images)
    (second_applied,) = call(
        functools.partial(far_kernel, pair), [flat], [], second_image, sign_live, tables, *arrived
    )
    multipliers, residual = call(
        functools.partial(end_kernel, pair), [((4, cases, pair), F32)] * 2,
        [pltpu.VMEM((4, cases, pair), F32)] * 2 + [pltpu.SemaphoreType.DMA((2,))],
        gathered, rhs, first, applied, second, second_applied, first_place=pltpu.HBM, later_place=pltpu.HBM,
    )
    return (multipliers[None, None], residual[None, None])


def solution(mesh):
    in_specs = (
        P("clus", "sub", None, None),
        P("clus", "sub", None, None, None),
        P("clus", "sub", None, None, None),
        P("clus", "sub", None),
        P("clus", "sub", None, None),
        P(),
    )
    out_specs = (P("clus", "sub", None, None, None), P("clus", "sub", None, None, None))
    return jax.shard_map(shards, mesh=mesh, in_specs=in_specs, out_specs=out_specs, check_vma=False)
```
